256 devices in a mesh: lat: 32 (over z, y), lon: 8 (over x, core).
Axes of the slice: x: 4, y: 4, z: 8, core: 2. Of those that a mesh axis runs over, the one named last changes fastest.
Arguments:
- grid_fields: bfloat16 [1280, 50, 3, 2560], P('lat', None, None, 'lon'), may hold values from -6 to 6
- legendre: bfloat16 [512, 1280, 640], P(('lat', 'lon')), may hold values from -0.15625 to 0.15625
- wave_of_slot: int32 [512], replicated, may hold values from 0 to 511, as said below
- energy_weight: float32 [3, 640], replicated, may hold values from 0.1 to 10
Outputs:
- spectral: bfloat16 [50, 3, 512, 2, 640], P(None, None, ('lat', 'lon'))
- gram_matrix: float32 [50, 50], replicated
The draws below stay inside these ranges and needn't reach their ends.
Inputs may be any that keep to these rules, and one draw needn't show every extreme that they name: `wave_of_slot`: every wavenumber 0 to 511 stands in exactly one slot; slot d * 2 + r holds a wavenumber of r * 256 to r * 256 + 255.
All inputs are finite; a program needn't handle non-finite values.
Results may differ from the reference program's by a relative error of at most 0.0043.
Values may be sent and summed in bfloat16 or wider, within the bound.
A program may use at most 128 MiB of HBM per device.

```python
import math
import jax
import jax.numpy as jnp
from jax import lax

NLAT = 1280
NLON = 2560
M = 512
NT = 640
K = 50
LEV = 3
WAVE_ROUND = 256
WAVE_DEV = 2


def draw_wave_of_slot(key, part):

    def draw_round(round_index):
        shuffled = jax.random.permutation(jax.random.fold_in(key, round_index), WAVE_ROUND)
        return shuffled.astype(jnp.int32) + round_index * WAVE_ROUND
    rounds = jax.vmap(draw_round)(jnp.arange(WAVE_DEV, dtype=jnp.int32))
    return rounds.T.reshape(M).astype(jnp.int32)


def shard_levels(stream_key, extent, cuts, least, top_value):
    loudness = 1.0
    for position, parts in cuts:
        heights = jax.random.uniform(jax.random.fold_in(jax.random.fold_in(stream_key, 6), position), (parts,), jnp.float32, least / len(cuts), top_value / len(cuts))
        loudness = loudness * jnp.repeat(jnp.exp(heights), extent[position] // parts).reshape((-1,) + (1,) * (len(extent) - 1 - position))
    return loudness


def scatter_about(own_key, dims, width, most, cuts=(), kind=jnp.bfloat16):
    entries = jax.random.normal(own_key, dims, jnp.float32) * width
    if len(cuts) > 0:
        entries = shard_levels(own_key, dims, cuts, -0.22, 0.18) * entries
    return jnp.clip(entries, min=-most, max=most).astype(kind)


def setup_inputs(seed: int = 0) -> dict:
    keys = jax.random.split(jax.random.key(seed), 5)
    grid_fields = scatter_about(keys[0], (NLAT, K, LEV, NLON), 1.0, 6.0, ((0, 32), (3, 8)))
    legendre = scatter_about(keys[1], (M, NLAT, NT), NLAT ** -0.5, 0.15625, ((0, 256),))
    wave_of_slot = draw_wave_of_slot(jax.random.fold_in(keys[4], 71), 0)
    energy_weight = jnp.clip(jnp.exp(jax.random.uniform(keys[3], (LEV, NT), jnp.float32, math.log(0.1), math.log(10.0))), 0.1, 10.0)
    return dict(grid_fields=grid_fields, legendre=legendre, wave_of_slot=wave_of_slot, energy_weight=energy_weight)


def make_trig(wave_list):
    longitude = jnp.arange(NLON, dtype=jnp.int32)
    phase_index = longitude[:, None] * wave_list.astype(jnp.int32)[None, :] % NLON
    angles = phase_index.astype(jnp.float32) * (2.0 * math.pi / NLON)
    stacked = jnp.stack([jnp.cos(angles), -jnp.sin(angles)], axis=2)
    return stacked.reshape(NLON, 2 * M).astype(jnp.bfloat16)

def reference(grid_fields, legendre, wave_of_slot, energy_weight):
    trig_table = make_trig(wave_of_slot)
    flat_rows = grid_fields.reshape(NLAT * K * LEV, NLON)
    fourier = jnp.dot(flat_rows, trig_table, preferred_element_type=jnp.float32) * (1.0 / math.sqrt(NLON))
    fourier = fourier.reshape(NLAT, K * LEV, M, 2)
    by_slot = jnp.moveaxis(fourier, 2, 0)
    degree_index = jnp.arange(NT, dtype=jnp.int32)
    tri_mask = (degree_index[None, :] >= wave_of_slot[:, None]).astype(jnp.float32)

    def per_slot(items):
        slot_data, slot_table, slot_mask = items
        masked = slot_table.astype(jnp.float32) * slot_mask[None, :]
        return jnp.einsum('afp,an->fpn', slot_data, masked, precision=lax.Precision.HIGHEST)
    full_slots = lax.map(per_slot, (by_slot, legendre, tri_mask))
    full = jnp.moveaxis(full_slots, 0, 1).reshape(K, LEV, M, 2, NT)
    factor = jnp.where(wave_of_slot == 0, 1.0, 2.0).astype(jnp.float32)
    weighted = full * factor[None, None, :, None, None] * energy_weight[None, :, None, None, :]
    gram_matrix = jnp.dot(full.reshape(K, -1), weighted.reshape(K, -1).T, precision=lax.Precision.HIGHEST)
    gram_matrix = gram_matrix / (LEV * M * NT)
    return (full.astype(jnp.bfloat16), gram_matrix)
```

```python
import math

import jax
import jax.numpy as jnp
from jax import lax
from jax.experimental import pallas as pl
from jax.experimental.pallas import tpu as pltpu
from jax.sharding import PartitionSpec as P

NLON = 2560
M = 512
NT = 640
LEV = 3
F32 = jnp.float32
BF16 = jnp.bfloat16
MESH = pl.DeviceIdType.MESH

CHUNKS = ((0, 2), (2, 2), (4, 1))
SIN_COEF = tuple(
    (-1) ** i * (math.pi / 2) ** (2 * i + 1) / math.factorial(2 * i + 1) for i in range(6)
)


def quarter_sine(z):
    square = z * z
    total = jnp.full_like(z, SIN_COEF[5])
    for coef in SIN_COEF[4::-1]:
        total = total * square + coef
    return total * z


def nt_dot(a, b, precision=None):
    return lax.dot_general(
        a, b, (((1,), (1,)), ((), ())), preferred_element_type=F32, precision=precision
    )


def kernel(
    x_ref, leg_hbm, wq_ref, wave_ref, ew_ref, spec_ref, gram_ref,
    xrs, xa, xrr, trig, xc, fb, sib, sb, rb, leg_v, leg32, legp, c32, ext32, amat, ost, wts,
    gs, ga, gb, gc,
    leg_sem, own_sem, s1_send, s1_recv, s1r_send, s1r_recv, sib_send, sib_recv,
    s2_send, s2_recv, g_send, g_recv,
):
    lat = lax.axis_index("lat")
    lon = lax.axis_index("lon")
    core = lax.rem(lon, 2)
    chip = lat * 4 + lon // 2

    leg_copy = pltpu.make_async_copy(leg_hbm, leg_v, leg_sem)
    leg_copy.start()

    def main_copy(c, peer):
        first, count = CHUNKS[c]
        return pltpu.make_async_remote_copy(
            src_ref=x_ref.at[pl.ds(peer * 5 + first, count), :, pl.ds(0, 256)],
            dst_ref=xa.at[pl.ds(first, count), :, pl.ds(pl.multiple_of(lon * 256, 256), 256)],
            send_sem=s1_send, recv_sem=s1_recv.at[c],
            device_id=(lat, peer), device_id_type=MESH,
        )

    def rest_copy(c, peer):
        first, count = CHUNKS[c]
        return pltpu.make_async_remote_copy(
            src_ref=xrs.at[pl.ds(peer * 5 + first, count)],
            dst_ref=xrr.at[lon, pl.ds(first, count)],
            send_sem=s1r_send, recv_sem=s1r_recv.at[c],
            device_id=(lat, peer), device_id_type=MESH,
        )

    def send_main(c):
        @pl.loop(1, 8)
        def _(k):
            main_copy(c, lax.rem(lon + k, 8)).start()

    def send_rest(c):
        @pl.loop(1, 8)
        def _(k):
            rest_copy(c, lax.rem(lon + k, 8)).start()

    send_main(0)
    lane_low = lax.broadcasted_iota(jnp.int32, (80, 128), 1) < 64

    @pl.loop(0, 40)
    def _(a):
        rest = x_ref[a, :, 256:320].astype(F32)
        xrs[a] = jnp.concatenate([rest[0:80], rest[80:160]], axis=1).astype(BF16)

    send_rest(0)
    for c in (1, 2):
        send_main(c)
        send_rest(c)
    own_main = pltpu.make_async_copy(
        x_ref.at[pl.ds(lon * 5, 5), :, pl.ds(0, 256)],
        xa.at[:, :, pl.ds(pl.multiple_of(lon * 256, 256), 256)],
        own_sem,
    )
    own_main.start()
    for i in range(5):
        xrr[lon, i] = xrs[lon * 5 + i]

    lane = lax.broadcasted_iota(jnp.int32, (1, 128), 1)

    @pl.loop(0, 4)
    def _(b):
        waves = jnp.transpose(jnp.broadcast_to(wq_ref[pl.ds(b, 1), :], (128, 128)))
        for t in range(20):
            if t < 16:
                place = lane + ((t // 2) * 320 + (t % 2) * 128)
            else:
                m = t - 16
                place = jnp.where(lane < 64, lane + (640 * m + 256), lane + (640 * m + 512))
            product = waves * place.astype(F32)
            turns = jnp.floor(product * (1.0 / NLON) + 0.5)
            phase = product - turns * NLON
            size = jnp.abs(phase)
            cosine = quarter_sine((640.0 - size) * (1.0 / 640.0))
            fold = 640.0 - jnp.abs(size - 640.0)
            sine = quarter_sine(jnp.where(phase < 0, fold, -fold) * (1.0 / 640.0))
            row = pl.multiple_of(b * 256, 256)
            trig[pl.ds(row, 128), t * 128:(t + 1) * 128] = cosine.astype(BF16)
            trig[pl.ds(row + 128, 128), t * 128:(t + 1) * 128] = sine.astype(BF16)

    leg_copy.wait()
    for r in range(2):
        @pl.loop(0, 10)
        def _(s):
            rows = pl.ds(pl.multiple_of(s * 128, 128), 128)
            for u in range(5):
                leg32[u, rows, :] = leg_v[r, rows, u * 128:(u + 1) * 128].astype(F32)

        for i in range(5):
            for u in range(5):
                legp[r, i * 256:(i + 1) * 256, u * 128:(u + 1) * 128] = leg32[
                    u, pl.ds(i, 256, stride=5), :
                ].astype(BF16)

    row_f = lax.broadcasted_iota(jnp.int32, (160, NT), 0).astype(F32)
    level = row_f - 3.0 * jnp.floor((row_f + 0.5) * (1.0 / 3.0))
    wts[...] = jnp.where(
        row_f > 149.5,
        0.0,
        jnp.where(
            level < 0.5,
            ew_ref[0:1, :],
            jnp.where(level < 1.5, ew_ref[1:2, :], ew_ref[2:3, :]),
        ),
    )

    own_main.wait()

    def to_sibling(c):
        return pltpu.make_async_remote_copy(
            src_ref=fb.at[c, 1 - core], dst_ref=sib.at[c],
            send_sem=sib_send.at[c], recv_sem=sib_recv.at[c],
            device_id=(lat, lon + 1 - 2 * core), device_id_type=MESH,
        )

    for c, (first, count) in enumerate(CHUNKS):
        window = xa.at[pl.ds(first, count), :, pl.ds(0, 1792)]
        pltpu.make_async_copy(window, window, s1_recv.at[c]).wait()
        window = xrr.at[pl.ds(0, 7), pl.ds(first, count)]
        pltpu.make_async_copy(window, window, s1r_recv.at[c]).wait()
        for i in range(first, first + count):
            for m in range(4):
                even = xrr[2 * m, i].astype(F32)
                odd = xrr[2 * m + 1, i].astype(F32)
                top = jnp.where(lane_low, even, pltpu.roll(odd, 64, 1))
                low = jnp.where(lane_low, pltpu.roll(even, 64, 1), odd)
                cols = slice(2048 + m * 128, 2176 + m * 128)
                xa[i, 0:80, cols] = top.astype(BF16)
                xa[i, 80:160, cols] = low.astype(BF16)
        for g in range(count):
            xc[g * 128:(g + 1) * 128, :] = xa[first + g, 0:128, :]
        if c == 2:
            dst = lax.broadcasted_iota(jnp.int32, (128, 160), 0)
            src = lax.broadcasted_iota(jnp.int32, (128, 160), 1)
            pick = jnp.zeros((128, 160), F32)
            for i in range(5):
                hit = (dst - 22 * i == src - 32 * i) & (dst >= 22 * i) & (dst < 22 * i + 22)
                pick = jnp.where(hit, 1.0, pick)
            pick = pick.astype(BF16)
            for t in range(5):
                cols = slice(t * 512, (t + 1) * 512)
                extra = jnp.concatenate([xa[i, 128:160, cols] for i in range(5)], axis=0)
                xc[128:256, cols] = jnp.dot(
                    pick, extra, preferred_element_type=F32
                ).astype(BF16)

        @pl.loop(0, 2)
        def _(h):
            side = lax.rem(core + 1 + h, 2)
            rows = pl.ds(pl.multiple_of(side * 512, 512), 512)
            product = nt_dot(trig[rows, :], xc[...]) * (1.0 / math.sqrt(NLON))
            for rp in range(4):
                for g in range(2):
                    fb[c, side, pl.ds(g * 4 + rp, 128, stride=8), :] = product[
                        rp * 128:(rp + 1) * 128, g * 128:(g + 1) * 128
                    ]

            @pl.when(h == 0)
            def _():
                to_sibling(c).start()

        to_sibling(c).wait_recv()

        @pl.loop(0, 8)
        def _(s):
            rows = pl.ds(pl.multiple_of(s * 128, 128), 128)
            mine = fb[c, core, rows, :].reshape(16, 8, 128)
            other = sib[c, rows, :].reshape(16, 8, 128)
            even = jnp.where(core == 0, mine, other)
            odd = jnp.where(core == 0, other, mine)
            sb[c, pl.ds(s * 16, 16)] = jnp.concatenate([even, odd], axis=1).astype(BF16)

        @pl.loop(1, 128)
        def _(k):
            target = lax.rem(chip + k * 37, 128)
            pltpu.make_async_remote_copy(
                src_ref=sb.at[c, target], dst_ref=rb.at[c, chip],
                send_sem=s2_send, recv_sem=s2_recv.at[c],
                device_id=(target // 4, lax.rem(target, 4) * 2 + core), device_id_type=MESH,
            ).start()

        rb[c, chip] = sb[c, chip]

    for c, (first, count) in enumerate(CHUNKS):
        window = rb.at[c, pl.ds(0, 127)]
        pltpu.make_async_copy(window, window, s2_recv.at[c]).wait()

        @pl.loop(0, 8)
        def _(s):
            c32[pl.ds(pl.multiple_of(s * 256, 256), 256), :] = (
                rb[c, pl.ds(s * 16, 16)].astype(F32).reshape(256, 128)
            )

        for r in range(2):
            for p in range(2):
                for g in range(2):
                    block = jnp.transpose(c32[pl.ds(g * 4 + r * 2 + p, 256, stride=8), :])
                    if g < count:
                        i = first + g
                        amat[r, p, 0:128, i * 256:(i + 1) * 256] = block.astype(BF16)
                    else:
                        ext32[...] = block
                        for i in range(5):
                            amat[r, p, 128:160, i * 256:(i + 1) * 256] = ext32[
                                22 * i:22 * i + 32, :
                            ].astype(BF16)

    degree = lax.broadcasted_iota(jnp.int32, (320, NT), 1)
    total = jnp.zeros((160, 160), F32)
    slot = (lat * 8 + lon) * 2
    for r in range(2):
        wave = wave_ref[slot + r]
        full = jnp.dot(
            amat[r].reshape(320, 1280), legp[r], preferred_element_type=F32
        )
        full = jnp.where(degree >= wave, full, 0.0)
        factor = jnp.where(wave == 0, 1.0, 2.0).astype(F32)
        for p in range(2):
            part = full[p * 160:(p + 1) * 160]
            for u in range(5):
                ost[u, pl.ds(r * 2 + p, 160, stride=4), :] = part[:, u * 128:(u + 1) * 128]
            total += nt_dot(part.astype(BF16), (part * (wts[...] * factor)).astype(BF16))

    row = lax.broadcasted_iota(jnp.int32, (160, 160), 0).astype(F32)
    col = lax.broadcasted_iota(jnp.int32, (160, 160), 1).astype(F32)
    row_mod = row - 3.0 * jnp.floor((row + 0.5) * (1.0 / 3.0))
    col_mod = col - 3.0 * jnp.floor((col + 0.5) * (1.0 / 3.0))
    total = jnp.where(row_mod == col_mod, total, 0.0)
    vec = lax.broadcasted_iota(jnp.int32, (128, 160), 0).astype(F32)
    src = lax.broadcasted_iota(jnp.int32, (128, 160), 1).astype(F32)
    pick = jnp.where(
        (jnp.floor((src + 0.5) * (1.0 / 3.0)) == vec) & (src < 149.5), 1.0, 0.0
    ).astype(F32)
    high = lax.Precision.HIGHEST
    half = jnp.dot(pick[0:64], total, preferred_element_type=F32, precision=high)
    gs[...] = (nt_dot(half, pick, high) * (1.0 / (LEV * M * NT))).reshape(8, 8, 128)

    def ring(which, src, dst):
        @pl.loop(1, 8)
        def _(k):
            peer = lax.rem(lon + k, 8)
            pltpu.make_async_remote_copy(
                src_ref=src(peer), dst_ref=dst.at[lon],
                send_sem=g_send.at[which], recv_sem=g_recv.at[which],
                device_id=(lat, peer), device_id_type=MESH,
            ).start()

    ring(0, lambda peer: gs.at[peer], ga)
    ga[lon] = gs[lon]
    for u in range(5):
        spec_ref[:, u * 128:(u + 1) * 128] = ost[u, 0:600, :].astype(BF16)
    pltpu.make_async_copy(ga.at[pl.ds(0, 7)], ga.at[pl.ds(0, 7)], g_recv.at[0]).wait()
    gb[lat] = jnp.sum(ga[...], axis=0)

    @pl.loop(1, 32)
    def _(k):
        peer = lax.rem(lat + k, 32)
        pltpu.make_async_remote_copy(
            src_ref=gb.at[lat], dst_ref=gb.at[lat],
            send_sem=g_send.at[1], recv_sem=g_recv.at[1],
            device_id=(peer, lon), device_id_type=MESH,
        ).start()

    pltpu.make_async_copy(gb.at[pl.ds(0, 31)], gb.at[pl.ds(0, 31)], g_recv.at[1]).wait()
    gc[lon] = jnp.sum(gb[...], axis=0)
    ring(2, lambda peer: gc.at[lon], gc)
    pltpu.make_async_copy(gc.at[pl.ds(0, 7)], gc.at[pl.ds(0, 7)], g_recv.at[2]).wait()
    gram_ref[...] = gc[...].reshape(64, 128)[0:50, 0:50]

    window = xa.at[:, :, pl.ds(0, 1792)]
    pltpu.make_async_copy(window, window, s1_send).wait()
    window = xrr.at[pl.ds(0, 7)]
    pltpu.make_async_copy(window, window, s1r_send).wait()
    for c in range(3):
        to_sibling(c).wait_send()
        window = rb.at[c, pl.ds(0, 127)]
        pltpu.make_async_copy(window, window, s2_send).wait()
    pltpu.make_async_copy(ga.at[pl.ds(0, 7)], ga.at[pl.ds(0, 7)], g_send.at[0]).wait()
    pltpu.make_async_copy(gb.at[pl.ds(0, 31)], gb.at[pl.ds(0, 31)], g_send.at[1]).wait()
    pltpu.make_async_copy(gc.at[pl.ds(0, 7)], gc.at[pl.ds(0, 7)], g_send.at[2]).wait()


def on_device(grid_fields, legendre, wave_of_slot, energy_weight):
    rows = jnp.pad(grid_fields.reshape(40, 150, 320), ((0, 0), (0, 10), (0, 0)))
    waves = wave_of_slot.reshape(128, 4).T.astype(F32)
    vmem = pl.BlockSpec(memory_space=pltpu.VMEM)
    dma = pltpu.SemaphoreType.DMA
    spectral, gram_matrix = pl.pallas_call(
        kernel,
        out_shape=(
            jax.ShapeDtypeStruct((600, NT), BF16),
            jax.ShapeDtypeStruct((50, 50), F32),
        ),
        in_specs=[
            vmem,
            pl.BlockSpec(memory_space=pl.ANY),
            vmem,
            pl.BlockSpec(memory_space=pltpu.SMEM),
            vmem,
        ],
        out_specs=(vmem, vmem),
        scratch_shapes=[
            pltpu.VMEM((40, 80, 128), BF16),
            pltpu.VMEM((5, 160, NLON), BF16),
            pltpu.VMEM((8, 5, 80, 128), BF16),
            pltpu.VMEM((1024, NLON), BF16),
            pltpu.VMEM((256, NLON), BF16),
            pltpu.VMEM((3, 2, 1024, 128), F32),
            pltpu.VMEM((3, 1024, 128), F32),
            pltpu.VMEM((3, 128, 16, 128), BF16),
            pltpu.VMEM((3, 128, 16, 128), BF16),
            pltpu.VMEM((2, 1280, NT), BF16),
            pltpu.VMEM((5, 1280, 128), F32),
            pltpu.VMEM((2, 1280, NT), BF16),
            pltpu.VMEM((2048, 128), F32),
            pltpu.VMEM((128, 256), F32),
            pltpu.VMEM((2, 2, 160, 1280), BF16),
            pltpu.VMEM((5, 640, 128), F32),
            pltpu.VMEM((160, NT), F32),
            pltpu.VMEM((8, 8, 128), F32),
            pltpu.VMEM((8, 8, 128), F32),
            pltpu.VMEM((32, 8, 128), F32),
            pltpu.VMEM((8, 8, 128), F32),
            dma, dma, dma, dma((3,)), dma, dma((3,)), dma((3,)), dma((3,)),
            dma, dma((3,)), dma((3,)), dma((3,)),
        ],
        compiler_params=pltpu.CompilerParams(
            has_side_effects=True, vmem_limit_bytes=56 * 1024 * 1024
        ),
        cost_estimate=pl.CostEstimate(
            flops=6_000_000_000, bytes_accessed=12_000_000, transcendentals=0
        ),
    )(rows, legendre, waves, wave_of_slot, energy_weight)
    return spectral.reshape(50, LEV, 2, 2, NT), gram_matrix


def solution(mesh):
    placed = (P("lat", None, None, "lon"), P(("lat", "lon"), None, None), P(), P())
    return jax.shard_map(
        on_device,
        mesh=mesh,
        in_specs=placed,
        out_specs=(P(None, None, ("lat", "lon"), None, None), P()),
        check_vma=False,
    )
```

```python
import math

import jax
import jax.numpy as jnp
from jax import lax
from jax.experimental import pallas as pl
from jax.experimental.pallas import tpu as pltpu
from jax.sharding import PartitionSpec as P

NLON = 2560
M = 512
NT = 640
LEV = 3
F32 = jnp.float32
BF16 = jnp.bfloat16
MESH = pl.DeviceIdType.MESH

EXTRA = 5
CHUNKS = ((EXTRA, 0), (1, 2), (3, 4))
STEP = 136
SIN_COEF = tuple(
    (-1) ** i * (math.pi / 2) ** (2 * i + 1) / math.factorial(2 * i + 1) for i in range(6)
)


def quarter_sine(z):
    square = z * z
    total = jnp.full_like(z, SIN_COEF[5])
    for coef in SIN_COEF[4::-1]:
        total = total * square + coef
    return total * z


def nt_dot(a, b, precision=None):
    return lax.dot_general(
        a, b, (((1,), (1,)), ((), ())), preferred_element_type=F32, precision=precision
    )


def kernel(
    x_hbm, leg_hbm, wq_ref, wave_ref, ew_ref, spec_ref, gram_ref,
    xv, x32, e32, xs, xrs, xa, xrr, trig, w32, fb, sib, sb, zb, rb, leg_v, leg32, legp,
    c32, ext32, amat, ost, wts, gs, ga, gb, gc,
    x_sem, leg_sem, own_sem, s1_send, s1_recv, s1r_send, s1r_recv, sib_send, sib_recv,
    zy_send, zy_recv, s2_send, s2_recv, g_send, g_recv,
):
    lat = lax.axis_index("lat")
    lon = lax.axis_index("lon")
    core = lax.rem(lon, 2)
    column = lon // 2

    def load_x(b):
        rows = pl.ds(32 * b, 32 if b < 4 else 22)
        return pltpu.make_async_copy(x_hbm.at[rows], xv.at[rows], x_sem.at[b])

    for b in range(5):
        load_x(b).start()
    leg_copy = pltpu.make_async_copy(leg_hbm, leg_v, leg_sem)
    leg_copy.start()

    barrier = pltpu.get_barrier_semaphore()

    @pl.loop(1, 8)
    def _(k):
        pl.semaphore_signal(
            barrier, inc=1, device_id=(lat, lax.rem(lon + k, 8)), device_id_type=MESH
        )

    @pl.loop(1, 32)
    def _(k):
        pl.semaphore_signal(
            barrier, inc=1, device_id=(lax.rem(lat + k, 32), lon), device_id_type=MESH
        )

    for t in range(3):
        e32[t] = jnp.zeros((968, 128), F32)
    for b in range(5):
        load_x(b).wait()

        @pl.loop(0, 32 if b < 4 else 22)
        def _(u):
            rows = xv[32 * b + u].astype(F32)
            for t in range(3):
                width = 128 if t < 2 else 64
                part = rows[:, t * 128:t * 128 + width]
                if b < 4:
                    x32[t, pl.ds(32 * b + u, 40, stride=STEP), 0:width] = part
                else:
                    e32[t, pl.ds(u, 40, stride=24), 0:width] = part

    pl.semaphore_wait(barrier, 38)

    def main_copy(c, peer):
        return pltpu.make_async_remote_copy(
            src_ref=xs.at[c, peer],
            dst_ref=xa.at[c, :, pl.ds(pl.multiple_of(lon * 256, 256), 256)],
            send_sem=s1_send, recv_sem=s1_recv.at[c],
            device_id=(lat, peer), device_id_type=MESH,
        )

    def rest_copy(c, peer):
        return pltpu.make_async_remote_copy(
            src_ref=xrs.at[c, peer], dst_ref=xrr.at[c, lon],
            send_sem=s1r_send, recv_sem=s1r_recv.at[c],
            device_id=(lat, peer), device_id_type=MESH,
        )

    low = lax.broadcasted_iota(jnp.int32, (128, 128), 1) < 64

    def pack(c, peer):
        def group(g, t):
            if CHUNKS[c][g] == EXTRA:
                return e32[t, pl.ds(pl.multiple_of(peer * 120, 8), 128), :]
            row = (peer * 5 + CHUNKS[c][g]) * STEP
            return x32[t, pl.ds(pl.multiple_of(row, 8), 128), :]

        for g in range(2):
            for t in range(2):
                xs[c, peer, g * 128:(g + 1) * 128, t * 128:(t + 1) * 128] = group(
                    g, t
                ).astype(BF16)
        rest = jnp.where(low, group(0, 2), pltpu.roll(group(1, 2), 64, 1))
        xrs[c, peer] = rest.astype(BF16)

    for c in range(3):
        @pl.loop(1, 8)
        def _(k):
            peer = lax.rem(lon + k, 8)
            pack(c, peer)
            main_copy(c, peer).start()
            rest_copy(c, peer).start()

    def own_copy(c):
        return pltpu.make_async_copy(
            xs.at[c, lon],
            xa.at[c, :, pl.ds(pl.multiple_of(lon * 256, 256), 256)],
            own_sem.at[c],
        )

    for c in range(3):
        pack(c, lon)
        own_copy(c).start()
        xrr[c, lon] = xrs[c, lon]

    lane = lax.broadcasted_iota(jnp.int32, (1, 128), 1)
    for b in range(4):
        w32[b * 128:(b + 1) * 128, :] = jnp.transpose(
            jnp.broadcast_to(wq_ref[b:b + 1, :].astype(F32), (128, 128))
        )

    @pl.loop(0, 4)
    def _(b):
        waves = w32[pl.ds(b, 128, stride=4), :]
        for t in range(20):
            if t < 16:
                place = lane + ((t // 2) * 320 + (t % 2) * 128)
            else:
                m = t - 16
                place = jnp.where(lane < 64, lane + (640 * m + 256), lane + (640 * m + 512))
            product = waves * place.astype(F32)
            turns = jnp.floor(product * (1.0 / NLON) + 0.5)
            phase = product - turns * NLON
            size = jnp.abs(phase)
            cosine = quarter_sine((640.0 - size) * (1.0 / 640.0))
            fold = 640.0 - jnp.abs(size - 640.0)
            sine = quarter_sine(jnp.where(phase < 0, fold, -fold) * (1.0 / 640.0))
            row = pl.multiple_of(b * 256, 256)
            trig[pl.ds(row, 128), t * 128:(t + 1) * 128] = cosine.astype(BF16)
            trig[pl.ds(row + 128, 128), t * 128:(t + 1) * 128] = sine.astype(BF16)

    leg_copy.wait()
    for r in range(2):
        @pl.loop(0, 10)
        def _(s):
            rows = pl.ds(pl.multiple_of(s * 128, 128), 128)
            for u in range(5):
                leg32[u, rows, :] = leg_v[r, rows, u * 128:(u + 1) * 128].astype(F32)

        for i in range(5):
            for u in range(5):
                legp[r, i * 256:(i + 1) * 256, u * 128:(u + 1) * 128] = leg32[
                    u, pl.ds(i, 256, stride=5), :
                ].astype(BF16)

    row_f = lax.broadcasted_iota(jnp.int32, (160, NT), 0).astype(F32)
    level = row_f - 3.0 * jnp.floor((row_f + 0.5) * (1.0 / 3.0))
    wts[...] = jnp.where(
        row_f > 149.5,
        0.0,
        jnp.where(
            level < 0.5,
            ew_ref[0:1, :],
            jnp.where(level < 1.5, ew_ref[1:2, :], ew_ref[2:3, :]),
        ),
    )

    def to_sibling(c):
        return pltpu.make_async_remote_copy(
            src_ref=fb.at[c, 1 - core], dst_ref=sib.at[c],
            send_sem=sib_send.at[c], recv_sem=sib_recv.at[c],
            device_id=(lat, lon + 1 - 2 * core), device_id_type=MESH,
        )

    def analyse(c):
        window = xa.at[c, :, pl.ds(0, 1792)]
        pltpu.make_async_copy(window, window, s1_recv.at[c]).wait()
        window = xrr.at[c, pl.ds(0, 7)]
        pltpu.make_async_copy(window, window, s1r_recv.at[c]).wait()
        own_copy(c).wait()
        for m in range(4):
            even = xrr[c, 2 * m].astype(F32)
            odd = xrr[c, 2 * m + 1].astype(F32)
            cols = slice(2048 + m * 128, 2176 + m * 128)
            xa[c, 0:128, cols] = jnp.where(low, even, pltpu.roll(odd, 64, 1)).astype(BF16)
            xa[c, 128:256, cols] = jnp.where(low, pltpu.roll(even, 64, 1), odd).astype(BF16)

        @pl.loop(0, 2)
        def _(h):
            side = lax.rem(core + 1 + h, 2)
            rows = pl.ds(pl.multiple_of(side * 512, 512), 512)
            product = nt_dot(trig[rows, :], xa[c]) * (1.0 / math.sqrt(NLON))
            for rp in range(4):
                for g in range(2):
                    fb[c, side, pl.ds(g * 4 + rp, 128, stride=8), :] = product[
                        rp * 128:(rp + 1) * 128, g * 128:(g + 1) * 128
                    ]

            @pl.when(h == 0)
            def _():
                to_sibling(c).start()

        to_sibling(c).wait_recv()

        @pl.loop(0, 8)
        def _(s):
            rows = pl.ds(pl.multiple_of(s * 128, 128), 128)
            mine = fb[c, core, rows, :].reshape(16, 8, 128)
            other = sib[c, rows, :].reshape(16, 8, 128)
            even = jnp.where(core == 0, mine, other)
            odd = jnp.where(core == 0, other, mine)
            both = jnp.concatenate([even, odd], axis=1).astype(BF16)
            sb[c, pl.ds(s * 4, 4)] = both.reshape(4, 4, 16, 128)

        @pl.loop(1, 32)
        def _(k):
            peer = lax.rem(lat + k, 32)
            pltpu.make_async_remote_copy(
                src_ref=sb.at[c, peer], dst_ref=zb.at[c, lat],
                send_sem=zy_send, recv_sem=zy_recv.at[c],
                device_id=(peer, lon), device_id_type=MESH,
            ).start()

        zb[c, lat] = sb[c, lat]

    def deliver(c):
        window = sb.at[c, pl.ds(0, 31)]
        pltpu.make_async_copy(window, window, zy_recv.at[c]).wait()

        @pl.loop(1, 4)
        def _(k):
            peer = lax.rem(column + k, 4)
            pltpu.make_async_remote_copy(
                src_ref=zb.at[c, :, peer], dst_ref=rb.at[c, :, column],
                send_sem=s2_send, recv_sem=s2_recv.at[c],
                device_id=(lat, peer * 2 + core), device_id_type=MESH,
            ).start()

        rb[c, :, column] = zb[c, :, column]

    def collect(c):
        window = rb.at[c, :, pl.ds(0, 3)]
        pltpu.make_async_copy(window, window, s2_recv.at[c]).wait()

        @pl.loop(0, 8)
        def _(s):
            c32[pl.ds(pl.multiple_of(s * 256, 256), 256), :] = (
                rb[c, pl.ds(s * 4, 4)].astype(F32).reshape(256, 128)
            )

        for r in range(2):
            for p in range(2):
                for g in range(2):
                    block = jnp.transpose(c32[pl.ds(g * 4 + r * 2 + p, 256, stride=8), :])
                    i = CHUNKS[c][g]
                    if i != EXTRA:
                        amat[r, p, 0:128, i * 256:(i + 1) * 256] = block.astype(BF16)
                    else:
                        ext32[...] = block
                        for i in range(5):
                            amat[r, p, 128:160, i * 256:(i + 1) * 256] = ext32[
                                24 * i:24 * i + 32, :
                            ].astype(BF16)

    analyse(0)
    analyse(1)
    deliver(0)
    analyse(2)
    deliver(1)
    collect(0)
    deliver(2)
    collect(1)
    collect(2)

    degree = lax.broadcasted_iota(jnp.int32, (320, NT), 1)
    total = jnp.zeros((160, 160), F32)
    slot = (lat * 8 + lon) * 2
    for r in range(2):
        wave = wave_ref[slot + r]
        full = jnp.dot(
            amat[r].reshape(320, 1280), legp[r], preferred_element_type=F32
        )
        full = jnp.where(degree >= wave, full, 0.0)
        factor = jnp.where(wave == 0, 1.0, 2.0).astype(F32)
        for p in range(2):
            part = full[p * 160:(p + 1) * 160]
            for u in range(5):
                ost[u, pl.ds(r * 2 + p, 160, stride=4), :] = part[:, u * 128:(u + 1) * 128]
            total += nt_dot(part.astype(BF16), (part * (wts[...] * factor)).astype(BF16))

    row = lax.broadcasted_iota(jnp.int32, (160, 160), 0).astype(F32)
    col = lax.broadcasted_iota(jnp.int32, (160, 160), 1).astype(F32)
    row_mod = row - 3.0 * jnp.floor((row + 0.5) * (1.0 / 3.0))
    col_mod = col - 3.0 * jnp.floor((col + 0.5) * (1.0 / 3.0))
    total = jnp.where(row_mod == col_mod, total, 0.0)
    vec = lax.broadcasted_iota(jnp.int32, (128, 160), 0).astype(F32)
    src = lax.broadcasted_iota(jnp.int32, (128, 160), 1).astype(F32)
    pick = jnp.where(
        (jnp.floor((src + 0.5) * (1.0 / 3.0)) == vec) & (src < 149.5), 1.0, 0.0
    ).astype(F32)
    high = lax.Precision.HIGHEST
    upper = jnp.where(
        (jnp.floor((src + 0.5) * (1.0 / 3.0)) == vec - 64.0) & (src < 149.5), 1.0, 0.0
    ).astype(F32)
    half = jnp.dot(pick[0:64], total, preferred_element_type=F32, precision=high)
    packed = nt_dot(half[0:32], pick, high) + nt_dot(half[32:64], upper, high)
    gs[...] = (packed * (1.0 / (LEV * M * NT))).reshape(8, 4, 128)

    def ring(which, src, dst):
        @pl.loop(1, 8)
        def _(k):
            peer = lax.rem(lon + k, 8)
            pltpu.make_async_remote_copy(
                src_ref=src(peer), dst_ref=dst.at[lon],
                send_sem=g_send.at[which], recv_sem=g_recv.at[which],
                device_id=(lat, peer), device_id_type=MESH,
            ).start()

    ring(0, lambda peer: gs.at[peer], ga)
    ga[lon] = gs[lon]
    for u in range(5):
        spec_ref[:, u * 128:(u + 1) * 128] = ost[u, 0:600, :].astype(BF16)
    pltpu.make_async_copy(ga.at[pl.ds(0, 7)], ga.at[pl.ds(0, 7)], g_recv.at[0]).wait()
    gb[lat] = jnp.sum(ga[...], axis=0)

    @pl.loop(1, 32)
    def _(k):
        peer = lax.rem(lat + k, 32)
        pltpu.make_async_remote_copy(
            src_ref=gb.at[lat], dst_ref=gb.at[lat],
            send_sem=g_send.at[1], recv_sem=g_recv.at[1],
            device_id=(peer, lon), device_id_type=MESH,
        ).start()

    pltpu.make_async_copy(gb.at[pl.ds(0, 31)], gb.at[pl.ds(0, 31)], g_recv.at[1]).wait()
    gc[lon] = jnp.sum(gb[...], axis=0)
    ring(2, lambda peer: gc.at[lon], gc)
    pltpu.make_async_copy(gc.at[pl.ds(0, 7)], gc.at[pl.ds(0, 7)], g_recv.at[2]).wait()
    packed = gc[...].reshape(32, 128)
    gram_ref[0:32, :] = packed[:, 0:50]
    gram_ref[32:50, :] = packed[0:18, 64:114]

    window = xa.at[:, :, pl.ds(0, 1792)]
    pltpu.make_async_copy(window, window, s1_send).wait()
    window = xrr.at[:, pl.ds(0, 7)]
    pltpu.make_async_copy(window, window, s1r_send).wait()
    for c in range(3):
        to_sibling(c).wait_send()
    window = sb.at[:, pl.ds(0, 31)]
    pltpu.make_async_copy(window, window, zy_send).wait()
    window = rb.at[:, :, pl.ds(0, 3)]
    pltpu.make_async_copy(window, window, s2_send).wait()
    pltpu.make_async_copy(ga.at[pl.ds(0, 7)], ga.at[pl.ds(0, 7)], g_send.at[0]).wait()
    pltpu.make_async_copy(gb.at[pl.ds(0, 31)], gb.at[pl.ds(0, 31)], g_send.at[1]).wait()
    pltpu.make_async_copy(gc.at[pl.ds(0, 7)], gc.at[pl.ds(0, 7)], g_send.at[2]).wait()


def on_device(grid_fields, legendre, wave_of_slot, energy_weight):
    rows = grid_fields.transpose(1, 2, 0, 3).reshape(150, 40, 320)
    waves = wave_of_slot.reshape(4, 128)
    vmem = pl.BlockSpec(memory_space=pltpu.VMEM)
    dma = pltpu.SemaphoreType.DMA
    spectral, gram_matrix = pl.pallas_call(
        kernel,
        out_shape=(
            jax.ShapeDtypeStruct((600, NT), BF16),
            jax.ShapeDtypeStruct((50, 50), F32),
        ),
        in_specs=[
            pl.BlockSpec(memory_space=pl.ANY),
            pl.BlockSpec(memory_space=pl.ANY),
            vmem,
            pl.BlockSpec(memory_space=pltpu.SMEM),
            vmem,
        ],
        out_specs=(vmem, vmem),
        scratch_shapes=[
            pltpu.VMEM((150, 40, 320), BF16),
            pltpu.VMEM((3, 40 * STEP, 128), F32),
            pltpu.VMEM((3, 968, 128), F32),
            pltpu.VMEM((3, 8, 256, 256), BF16),
            pltpu.VMEM((3, 8, 128, 128), BF16),
            pltpu.VMEM((3, 256, NLON), BF16),
            pltpu.VMEM((3, 8, 128, 128), BF16),
            pltpu.VMEM((1024, NLON), BF16),
            pltpu.VMEM((512, 128), F32),
            pltpu.VMEM((3, 2, 1024, 128), F32),
            pltpu.VMEM((3, 1024, 128), F32),
            pltpu.VMEM((3, 32, 4, 16, 128), BF16),
            pltpu.VMEM((3, 32, 4, 16, 128), BF16),
            pltpu.VMEM((3, 32, 4, 16, 128), BF16),
            pltpu.VMEM((2, 1280, NT), BF16),
            pltpu.VMEM((5, 1280, 128), F32),
            pltpu.VMEM((2, 1280, NT), BF16),
            pltpu.VMEM((2048, 128), F32),
            pltpu.VMEM((128, 256), F32),
            pltpu.VMEM((2, 2, 160, 1280), BF16),
            pltpu.VMEM((5, 640, 128), F32),
            pltpu.VMEM((160, NT), F32),
            pltpu.VMEM((8, 4, 128), F32),
            pltpu.VMEM((8, 4, 128), F32),
            pltpu.VMEM((32, 4, 128), F32),
            pltpu.VMEM((8, 4, 128), F32),
            dma((5,)), dma, dma((3,)), dma, dma((3,)), dma, dma((3,)), dma((3,)), dma((3,)),
            dma, dma((3,)), dma, dma((3,)), dma((3,)), dma((3,)),
        ],
        compiler_params=pltpu.CompilerParams(
            collective_id=0, has_side_effects=True, vmem_limit_bytes=60 * 1024 * 1024,
        ),
        cost_estimate=pl.CostEstimate(
            flops=6_000_000_000, bytes_accessed=12_000_000, transcendentals=0
        ),
    )(rows, legendre, waves, wave_of_slot, energy_weight)
    return spectral.reshape(50, LEV, 2, 2, NT), gram_matrix


def solution(mesh):
    placed = (P("lat", None, None, "lon"), P(("lat", "lon"), None, None), P(), P())
    return jax.shard_map(
        on_device,
        mesh=mesh,
        in_specs=placed,
        out_specs=(P(None, None, ("lat", "lon"), None, None), P()),
        check_vma=False,
    )
```

```python
import math

import jax
import jax.numpy as jnp
from jax import lax
from jax.experimental import pallas as pl
from jax.experimental.pallas import tpu as pltpu
from jax.sharding import PartitionSpec as P

NLON = 2560
M = 512
NT = 640
LEV = 3
F32 = jnp.float32
BF16 = jnp.bfloat16
MESH = pl.DeviceIdType.MESH

FG = 25
CHUNKS = ((0, 2), (2, 2), (4, 1), (5, 1))
SIN_COEF = tuple(
    (-1) ** i * (math.pi / 2) ** (2 * i + 1) / math.factorial(2 * i + 1) for i in range(6)
)


def quarter_sine(z):
    square = z * z
    total = jnp.full_like(z, SIN_COEF[5])
    for coef in SIN_COEF[4::-1]:
        total = total * square + coef
    return total * z


def nt_dot(a, b, precision=None):
    return lax.dot_general(
        a, b, (((1,), (1,)), ((), ())), preferred_element_type=F32, precision=precision
    )


def kernel(
    x_hbm, leg_hbm, wq_ref, wave_ref, ew_ref, spec_ref, gram_ref,
    xv, x32, xs, xrs, xa, xrr, trig, wn, w32, sb, zb, r32, rbs, rb, leg_v, leg32, legp,
    c32, ext32, amat, out, ost, wts, gs, ga, gb, gc,
    x_sem, leg_sem, own_sem, s1_send, s1_recv, s1r_send, s1r_recv,
    zy_send, zy_recv, s2_send, s2_recv, g_send, g_recv,
):
    lat = lax.axis_index("lat")
    lon = lax.axis_index("lon")

    def load_x(g):
        rows = pl.ds(FG * g, FG)
        return pltpu.make_async_copy(x_hbm.at[rows], xv.at[rows], x_sem.at[g])

    for g in range(6):
        load_x(g).start()
    leg_copy = pltpu.make_async_copy(leg_hbm, leg_v, leg_sem)
    leg_copy.start()

    barrier = pltpu.get_barrier_semaphore()

    @pl.loop(1, 8)
    def _(k):
        pl.semaphore_signal(
            barrier, inc=1, device_id=(lat, lax.rem(lon + k, 8)), device_id_type=MESH
        )

    @pl.loop(1, 32)
    def _(k):
        pl.semaphore_signal(
            barrier, inc=1, device_id=(lax.rem(lat + k, 32), lon), device_id_type=MESH
        )

    x32[:, :, 1000:1008, :] = jnp.zeros((6, 3, 8, 128), F32)
    ext32[128:136, :] = jnp.zeros((8, 256), F32)

    def relay(g):
        load_x(g).wait()

        @pl.loop(0, FG)
        def _(u):
            rows = xv[FG * g + u].astype(F32)
            for t in range(3):
                width = 128 if t < 2 else 64
                x32[g, t, pl.ds(u, 40, stride=FG), 0:width] = rows[
                    :, t * 128:t * 128 + width
                ]

    def main_copy(c, peer):
        first, count = CHUNKS[c]
        rows = pl.ds(first * 128, count * 128)
        return pltpu.make_async_remote_copy(
            src_ref=xs.at[peer, rows],
            dst_ref=xa.at[rows, pl.ds(pl.multiple_of(lon * 256, 256), 256)],
            send_sem=s1_send, recv_sem=s1_recv.at[c],
            device_id=(lat, peer), device_id_type=MESH,
        )

    def rest_copy(c, peer):
        first, count = CHUNKS[c]
        rows = pl.ds(first * 64, count * 64)
        return pltpu.make_async_remote_copy(
            src_ref=xrs.at[peer, rows], dst_ref=xrr.at[lon, rows],
            send_sem=s1r_send, recv_sem=s1r_recv.at[c],
            device_id=(lat, peer), device_id_type=MESH,
        )

    low = lax.broadcasted_iota(jnp.int32, (64, 128), 1) < 64

    def pack(c, peer):
        first, count = CHUNKS[c]
        for g in range(first, first + count):
            for t in range(2):
                xs[peer, g * 128:(g + 1) * 128, t * 128:(t + 1) * 128] = x32[
                    g, t, pl.ds(peer * 125, 128), :
                ].astype(BF16)
            rest = x32[g, 2, pl.ds(peer * 125, 128), :]
            rest = jnp.where(low, rest[0:64], pltpu.roll(rest[64:128], 64, 1))
            xrs[peer, g * 64:(g + 1) * 64, :] = rest.astype(BF16)

    def own_copy(c):
        first, count = CHUNKS[c]
        rows = pl.ds(first * 128, count * 128)
        return pltpu.make_async_copy(
            xs.at[lon, rows],
            xa.at[rows, pl.ds(pl.multiple_of(lon * 256, 256), 256)],
            own_sem.at[c],
        )

    for c, (first, count) in enumerate(CHUNKS):
        for g in range(first, first + count):
            relay(g)
        if c == 0:
            pl.semaphore_wait(barrier, 38)

        @pl.loop(1, 8)
        def _(k):
            peer = lax.rem(lon + k, 8)
            pack(c, peer)
            main_copy(c, peer).start()
            rest_copy(c, peer).start()

    for c, (first, count) in enumerate(CHUNKS):
        pack(c, lon)
        own_copy(c).start()
        for g in range(first, first + count):
            xrr[lon, g * 64:(g + 1) * 64, :] = xrs[lon, g * 64:(g + 1) * 64, :]

    lane = lax.broadcasted_iota(jnp.int32, (1, 128), 1)
    for b in range(4):
        wn[b * 128:(b + 1) * 128, :] = jnp.transpose(
            jnp.broadcast_to(wq_ref[b:b + 1, :].astype(F32), (128, 128))
        )

    @pl.loop(0, 32)
    def _(z):
        for r in range(2):
            w32[pl.ds(pl.multiple_of(z * 16 + r * 8, 8), 8), :] = wn[
                pl.ds(z * 16 + r, 8, stride=2), :
            ]

    @pl.loop(0, 8)
    def _(b):
        waves = w32[pl.ds(pl.multiple_of(b * 64, 64), 64), :]
        for t in range(20):
            if t < 16:
                place = lane + ((t // 2) * 320 + (t % 2) * 128)
            else:
                m = t - 16
                place = jnp.where(lane < 64, lane + (640 * m + 256), lane + (640 * m + 512))
            product = waves * place.astype(F32)
            turns = jnp.floor(product * (1.0 / NLON) + 0.5)
            phase = product - turns * NLON
            size = jnp.abs(phase)
            cosine = quarter_sine((640.0 - size) * (1.0 / 640.0))
            fold = 640.0 - jnp.abs(size - 640.0)
            sine = quarter_sine(jnp.where(phase < 0, fold, -fold) * (1.0 / 640.0))
            pair = jnp.concatenate(
                [cosine.reshape(8, 8, 128), sine.reshape(8, 8, 128)], axis=1
            ).reshape(128, 128)
            trig[pl.ds(pl.multiple_of(b * 128, 128), 128), t * 128:(t + 1) * 128] = (
                pair.astype(BF16)
            )

    leg_copy.wait()
    for r in range(2):
        @pl.loop(0, 10)
        def _(s):
            rows = pl.ds(pl.multiple_of(s * 128, 128), 128)
            for u in range(5):
                leg32[u, rows, :] = leg_v[r, rows, u * 128:(u + 1) * 128].astype(F32)

        @pl.loop(0, 8)
        def _(j):
            for i in range(5):
                for u in range(5):
                    rows = pl.ds(pl.multiple_of(i * 256 + j * 32, 32), 32)
                    legp[r, rows, u * 128:(u + 1) * 128] = leg32[
                        u, pl.ds(j * 5 + i, 32, stride=40), :
                    ].astype(BF16)

    def fields_of(shape, axis):
        row = lax.broadcasted_iota(jnp.int32, shape, axis).astype(F32)
        group = jnp.floor((row + 0.5) * (1.0 / 32.0))
        within = row - 32.0 * group
        field = float(FG) * group + within
        vector = jnp.floor((field + 0.5) * (1.0 / 3.0))
        return within < FG - 0.5, vector, field - 3.0 * vector

    used, _, level = fields_of((192, NT), 0)
    wts[...] = jnp.where(
        used,
        jnp.where(
            level < 0.5,
            ew_ref[0:1, :],
            jnp.where(level < 1.5, ew_ref[1:2, :], ew_ref[2:3, :]),
        ),
        0.0,
    )

    def analyse(c):
        first, count = CHUNKS[c]
        window = xa.at[pl.ds(first * 128, count * 128), pl.ds(0, 1792)]
        pltpu.make_async_copy(window, window, s1_recv.at[c]).wait()
        window = xrr.at[pl.ds(0, 7), pl.ds(first * 64, count * 64)]
        pltpu.make_async_copy(window, window, s1r_recv.at[c]).wait()
        own_copy(c).wait()
        for g in range(first, first + count):
            for m in range(4):
                even = xrr[2 * m, g * 64:(g + 1) * 64, :].astype(F32)
                odd = xrr[2 * m + 1, g * 64:(g + 1) * 64, :].astype(F32)
                cols = slice(2048 + m * 128, 2176 + m * 128)
                xa[g * 128:g * 128 + 64, cols] = jnp.where(
                    low, even, pltpu.roll(odd, 64, 1)
                ).astype(BF16)
                xa[g * 128 + 64:g * 128 + 128, cols] = jnp.where(
                    low, pltpu.roll(even, 64, 1), odd
                ).astype(BF16)

        @pl.loop(0, 2)
        def _(h):
            half = lax.rem(lat // 16 + 1 + h, 2)
            rows = pl.ds(pl.multiple_of(half * 512, 512), 512)
            product = nt_dot(trig[rows, :], xa[first * 128:(first + count) * 128, :])
            product = (product * (1.0 / math.sqrt(NLON))).astype(BF16)
            for g in range(count):
                sb[first + g, pl.ds(half * 16, 16)] = product[
                    :, g * 128:(g + 1) * 128
                ].reshape(16, 32, 128)

            @pl.loop(0, 16)
            def _(k):
                peer = half * 16 + lax.rem(lat + k + 8, 16)

                @pl.when(peer != lat)
                def _():
                    pltpu.make_async_remote_copy(
                        src_ref=sb.at[pl.ds(first, count), peer],
                        dst_ref=zb.at[pl.ds(first, count), lat],
                        send_sem=zy_send, recv_sem=zy_recv.at[c],
                        device_id=(peer, lon), device_id_type=MESH,
                    ).start()

        for g in range(first, first + count):
            zb[g, lat] = sb[g, lat]

    def deliver(c):
        first, count = CHUNKS[c]
        window = sb.at[pl.ds(first, count), pl.ds(0, 31)]
        pltpu.make_async_copy(window, window, zy_recv.at[c]).wait()
        for g in range(first, first + count):
            @pl.loop(0, 8)
            def _(s):
                for e in range(4):
                    rows = zb[g, s * 4 + e].astype(F32)
                    for rp in range(4):
                        r32[pl.ds(s * 16 + e * 4 + rp, 8, stride=136), :] = rows[
                            rp * 8:(rp + 1) * 8
                        ]

            for j in range(8):
                rbs[g, j] = r32[j * 136:j * 136 + 128, :].astype(BF16)

        @pl.loop(1, 8)
        def _(k):
            peer = lax.rem(lon + k, 8)
            pltpu.make_async_remote_copy(
                src_ref=rbs.at[pl.ds(first, count), peer],
                dst_ref=rb.at[pl.ds(first, count), lon],
                send_sem=s2_send, recv_sem=s2_recv.at[c],
                device_id=(lat, peer), device_id_type=MESH,
            ).start()

        for g in range(first, first + count):
            rb[g, lon] = rbs[g, lon]

    slot = (lat * 8 + lon) * 2

    def collect(c):
        first, count = CHUNKS[c]
        window = rb.at[pl.ds(first, count), pl.ds(0, 7)]
        pltpu.make_async_copy(window, window, s2_recv.at[c]).wait()
        for g in range(first, first + count):
            @pl.loop(0, 8)
            def _(j):
                c32[pl.ds(pl.multiple_of(j * 128, 128), 128), :] = rb[g, j].astype(F32)

            for r in range(2):
                for p in range(2):
                    ext32[0:128, :] = jnp.transpose(c32[pl.ds(r * 2 + p, 256, stride=4), :])
                    for i in range(5):
                        amat[r, p, g * 32:(g + 1) * 32, i * 256:(i + 1) * 256] = ext32[
                            FG * i:FG * i + 32, :
                        ].astype(BF16)
        rows = slice(first * 32, (first + count) * 32)
        degree = lax.broadcasted_iota(jnp.int32, (count * 64, NT), 1)
        for r in range(2):
            full = jnp.dot(
                amat[r, :, rows, :].reshape(count * 64, 1280), legp[r],
                preferred_element_type=F32,
            )
            full = jnp.where(degree >= wave_ref[slot + r], full, 0.0)
            for p in range(2):
                part = full[p * count * 32:(p + 1) * count * 32]
                out[r, p, rows, :] = part
                for g in range(count):
                    start = 4 * FG * (first + g) + r * 2 + p
                    for u in range(5):
                        ost[u, pl.ds(start, 32, stride=4), :] = part[
                            g * 32:(g + 1) * 32, u * 128:(u + 1) * 128
                        ]

    analyse(0)
    analyse(1)
    analyse(2)
    deliver(0)
    analyse(3)
    deliver(1)
    collect(0)
    deliver(2)
    collect(1)
    deliver(3)
    collect(2)
    collect(3)

    total = jnp.zeros((192, 192), F32)
    for r in range(2):
        factor = jnp.where(wave_ref[slot + r] == 0, 1.0, 2.0).astype(F32)
        for p in range(2):
            part = out[r, p]
            total += nt_dot(part.astype(BF16), (part * (wts[...] * factor)).astype(BF16))

    _, _, row_level = fields_of((192, 192), 0)
    _, _, col_level = fields_of((192, 192), 1)
    total = jnp.where(row_level == col_level, total, 0.0)
    vec = lax.broadcasted_iota(jnp.int32, (128, 192), 0).astype(F32)
    used, vector, _ = fields_of((128, 192), 1)
    pick = jnp.where(used & (vector == vec), 1.0, 0.0).astype(F32)
    upper = jnp.where(used & (vector == vec - 64.0), 1.0, 0.0).astype(F32)
    high = lax.Precision.HIGHEST
    half = jnp.dot(pick[0:64], total, preferred_element_type=F32, precision=high)
    packed = nt_dot(half[0:32], pick, high) + nt_dot(half[32:64], upper, high)
    gs[...] = (packed * (1.0 / (LEV * M * NT))).reshape(8, 4, 128)

    def ring(which, src, dst):
        @pl.loop(1, 8)
        def _(k):
            peer = lax.rem(lon + k, 8)
            pltpu.make_async_remote_copy(
                src_ref=src(peer), dst_ref=dst.at[lon],
                send_sem=g_send.at[which], recv_sem=g_recv.at[which],
                device_id=(lat, peer), device_id_type=MESH,
            ).start()

    ring(0, lambda peer: gs.at[peer], ga)
    ga[lon] = gs[lon]
    for u in range(5):
        spec_ref[:, u * 128:(u + 1) * 128] = ost[u, 0:600, :].astype(BF16)
    pltpu.make_async_copy(ga.at[pl.ds(0, 7)], ga.at[pl.ds(0, 7)], g_recv.at[0]).wait()
    gb[lat] = jnp.sum(ga[...], axis=0)

    @pl.loop(1, 32)
    def _(k):
        peer = lax.rem(lat + 1 + lax.rem(k + 11, 31), 32)
        pltpu.make_async_remote_copy(
            src_ref=gb.at[lat], dst_ref=gb.at[lat],
            send_sem=g_send.at[1], recv_sem=g_recv.at[1],
            device_id=(peer, lon), device_id_type=MESH,
        ).start()

    pltpu.make_async_copy(gb.at[pl.ds(0, 31)], gb.at[pl.ds(0, 31)], g_recv.at[1]).wait()
    gc[lon] = jnp.sum(gb[...], axis=0)
    ring(2, lambda peer: gc.at[lon], gc)
    pltpu.make_async_copy(gc.at[pl.ds(0, 7)], gc.at[pl.ds(0, 7)], g_recv.at[2]).wait()
    packed = gc[...].reshape(32, 128)
    gram_ref[0:32, :] = packed[:, 0:50]
    gram_ref[32:50, :] = packed[0:18, 64:114]

    window = xa.at[:, pl.ds(0, 1792)]
    pltpu.make_async_copy(window, window, s1_send).wait()
    window = xrr.at[pl.ds(0, 7)]
    pltpu.make_async_copy(window, window, s1r_send).wait()
    window = sb.at[:, pl.ds(0, 31)]
    pltpu.make_async_copy(window, window, zy_send).wait()
    window = rb.at[:, pl.ds(0, 7)]
    pltpu.make_async_copy(window, window, s2_send).wait()
    pltpu.make_async_copy(ga.at[pl.ds(0, 7)], ga.at[pl.ds(0, 7)], g_send.at[0]).wait()
    pltpu.make_async_copy(gb.at[pl.ds(0, 31)], gb.at[pl.ds(0, 31)], g_send.at[1]).wait()
    pltpu.make_async_copy(gc.at[pl.ds(0, 7)], gc.at[pl.ds(0, 7)], g_send.at[2]).wait()


def on_device(grid_fields, legendre, wave_of_slot, energy_weight):
    rows = grid_fields.transpose(1, 2, 0, 3).reshape(150, 40, 320)
    waves = wave_of_slot.reshape(4, 128)
    vmem = pl.BlockSpec(memory_space=pltpu.VMEM)
    dma = pltpu.SemaphoreType.DMA
    many = dma((len(CHUNKS),))
    spectral, gram_matrix = pl.pallas_call(
        kernel,
        out_shape=(
            jax.ShapeDtypeStruct((600, NT), BF16),
            jax.ShapeDtypeStruct((50, 50), F32),
        ),
        in_specs=[
            pl.BlockSpec(memory_space=pl.ANY),
            pl.BlockSpec(memory_space=pl.ANY),
            vmem,
            pl.BlockSpec(memory_space=pltpu.SMEM),
            vmem,
        ],
        out_specs=(vmem, vmem),
        scratch_shapes=[
            pltpu.VMEM((150, 40, 320), BF16),
            pltpu.VMEM((6, 3, 1008, 128), F32),
            pltpu.VMEM((8, 768, 256), BF16),
            pltpu.VMEM((8, 384, 128), BF16),
            pltpu.VMEM((768, NLON), BF16),
            pltpu.VMEM((8, 384, 128), BF16),
            pltpu.VMEM((1024, NLON), BF16),
            pltpu.VMEM((512, 128), F32),
            pltpu.VMEM((512, 128), F32),
            pltpu.VMEM((6, 32, 32, 128), BF16),
            pltpu.VMEM((6, 32, 32, 128), BF16),
            pltpu.VMEM((8 * 136, 128), F32),
            pltpu.VMEM((6, 8, 128, 128), BF16),
            pltpu.VMEM((6, 8, 128, 128), BF16),
            pltpu.VMEM((2, 1280, NT), BF16),
            pltpu.VMEM((5, 1280, 128), F32),
            pltpu.VMEM((2, 1280, NT), BF16),
            pltpu.VMEM((1024, 128), F32),
            pltpu.VMEM((136, 256), F32),
            pltpu.VMEM((2, 2, 192, 1280), BF16),
            pltpu.VMEM((2, 2, 192, NT), F32),
            pltpu.VMEM((5, 632, 128), F32),
            pltpu.VMEM((192, NT), F32),
            pltpu.VMEM((8, 4, 128), F32),
            pltpu.VMEM((8, 4, 128), F32),
            pltpu.VMEM((32, 4, 128), F32),
            pltpu.VMEM((8, 4, 128), F32),
            dma((6,)), dma, many, dma, many, dma, many,
            dma, many, dma, many, dma((3,)), dma((3,)),
        ],
        compiler_params=pltpu.CompilerParams(
            collective_id=0, has_side_effects=True, vmem_limit_bytes=60 * 1024 * 1024,
        ),
        cost_estimate=pl.CostEstimate(
            flops=6_000_000_000, bytes_accessed=12_000_000, transcendentals=0
        ),
    )(rows, legendre, waves, wave_of_slot, energy_weight)
    return spectral.reshape(50, LEV, 2, 2, NT), gram_matrix


def solution(mesh):
    placed = (P("lat", None, None, "lon"), P(("lat", "lon"), None, None), P(), P())
    return jax.shard_map(
        on_device,
        mesh=mesh,
        in_specs=placed,
        out_specs=(P(None, None, ("lat", "lon"), None, None), P()),
        check_vma=False,
    )
```

```python
import math

import jax
import jax.numpy as jnp
from jax import lax
from jax.experimental import pallas as pl
from jax.experimental.pallas import tpu as pltpu
from jax.sharding import PartitionSpec as P

NLON = 2560
M = 512
NT = 640
LEV = 3
F32 = jnp.float32
BF16 = jnp.bfloat16
MESH = pl.DeviceIdType.MESH

FG = 25
CHUNKS = ((0, 1), (1, 2), (3, 1), (4, 1), (5, 1))
SIN_COEF = tuple(
    (-1) ** i * (math.pi / 2) ** (2 * i + 1) / math.factorial(2 * i + 1) for i in range(6)
)


def quarter_sine(z):
    square = z * z
    total = jnp.full_like(z, SIN_COEF[5])
    for coef in SIN_COEF[4::-1]:
        total = total * square + coef
    return total * z


def nt_dot(a, b, precision=None):
    return lax.dot_general(
        a, b, (((1,), (1,)), ((), ())), preferred_element_type=F32, precision=precision
    )


def kernel(
    x_hbm, leg_hbm, wq_ref, wave_ref, ew_ref, spec_ref, gram_ref,
    xv, x32, xs, xrs, xa, xrr, trig, wn, w32, sb, zb, r32, rbs, rb, leg_v, leg32, legp,
    c32, ext32, amat, out, ost, wts, spec_v, gs, ga, gb, gc,
    x_sem, leg_sem, spec_sem, own_sem, s1_send, s1_recv, s1r_send, s1r_recv,
    zy_send, zy_recv, s2_send, s2_recv, g_send, g_recv,
):
    lat = lax.axis_index("lat")
    lon = lax.axis_index("lon")

    def load_x(g):
        rows = pl.ds(FG * g, FG)
        return pltpu.make_async_copy(x_hbm.at[rows], xv.at[rows], x_sem.at[g])

    for g in range(6):
        load_x(g).start()
    leg_copy = pltpu.make_async_copy(leg_hbm, leg_v, leg_sem)
    leg_copy.start()

    barrier = pltpu.get_barrier_semaphore()

    @pl.loop(1, 8)
    def _(k):
        pl.semaphore_signal(
            barrier, inc=1, device_id=(lat, lax.rem(lon + k, 8)), device_id_type=MESH
        )

    @pl.loop(1, 32)
    def _(k):
        pl.semaphore_signal(
            barrier, inc=1, device_id=(lax.rem(lat + k, 32), lon), device_id_type=MESH
        )

    x32[:, :, 1000:1008, :] = jnp.zeros((6, 3, 8, 128), F32)
    ext32[128:136, :] = jnp.zeros((8, 256), F32)

    def relay(g):
        load_x(g).wait()

        @pl.loop(0, FG)
        def _(u):
            rows = xv[FG * g + u].astype(F32)
            for t in range(3):
                width = 128 if t < 2 else 64
                x32[g, t, pl.ds(u, 40, stride=FG), 0:width] = rows[
                    :, t * 128:t * 128 + width
                ]

    def main_copy(c, peer):
        first, count = CHUNKS[c]
        rows = pl.ds(first * 128, count * 128)
        return pltpu.make_async_remote_copy(
            src_ref=xs.at[peer, rows],
            dst_ref=xa.at[rows, pl.ds(pl.multiple_of(lon * 256, 256), 256)],
            send_sem=s1_send, recv_sem=s1_recv.at[c],
            device_id=(lat, peer), device_id_type=MESH,
        )

    def rest_copy(c, peer):
        first, count = CHUNKS[c]
        rows = pl.ds(first * 64, count * 64)
        return pltpu.make_async_remote_copy(
            src_ref=xrs.at[peer, rows], dst_ref=xrr.at[lon, rows],
            send_sem=s1r_send, recv_sem=s1r_recv.at[c],
            device_id=(lat, peer), device_id_type=MESH,
        )

    low = lax.broadcasted_iota(jnp.int32, (64, 128), 1) < 64

    def pack(c, peer):
        first, count = CHUNKS[c]
        for g in range(first, first + count):
            for t in range(2):
                xs[peer, g * 128:(g + 1) * 128, t * 128:(t + 1) * 128] = x32[
                    g, t, pl.ds(peer * 125, 128), :
                ].astype(BF16)
            rest = x32[g, 2, pl.ds(peer * 125, 128), :]
            rest = jnp.where(low, rest[0:64], pltpu.roll(rest[64:128], 64, 1))
            xrs[peer, g * 64:(g + 1) * 64, :] = rest.astype(BF16)

    def own_copy(c):
        first, count = CHUNKS[c]
        rows = pl.ds(first * 128, count * 128)
        return pltpu.make_async_copy(
            xs.at[lon, rows],
            xa.at[rows, pl.ds(pl.multiple_of(lon * 256, 256), 256)],
            own_sem.at[c],
        )

    for c, (first, count) in enumerate(CHUNKS):
        for g in range(first, first + count):
            relay(g)
        if c == 0:
            pl.semaphore_wait(barrier, 38)

        @pl.loop(1, 8)
        def _(k):
            peer = lax.rem(lon + k, 8)
            pack(c, peer)
            main_copy(c, peer).start()
            rest_copy(c, peer).start()

    for c, (first, count) in enumerate(CHUNKS):
        pack(c, lon)
        own_copy(c).start()
        for g in range(first, first + count):
            xrr[lon, g * 64:(g + 1) * 64, :] = xrs[lon, g * 64:(g + 1) * 64, :]

    lane = lax.broadcasted_iota(jnp.int32, (1, 128), 1)
    for b in range(4):
        wn[b * 128:(b + 1) * 128, :] = jnp.transpose(
            jnp.broadcast_to(wq_ref[b:b + 1, :].astype(F32), (128, 128))
        )

    @pl.loop(0, 32)
    def _(z):
        for r in range(2):
            w32[pl.ds(pl.multiple_of(z * 16 + r * 8, 8), 8), :] = wn[
                pl.ds(z * 16 + r, 8, stride=2), :
            ]

    @pl.loop(0, 8)
    def _(b):
        waves = w32[pl.ds(pl.multiple_of(b * 64, 64), 64), :]
        for t in range(20):
            if t < 16:
                place = lane + ((t // 2) * 320 + (t % 2) * 128)
            else:
                m = t - 16
                place = jnp.where(lane < 64, lane + (640 * m + 256), lane + (640 * m + 512))
            product = waves * place.astype(F32)
            turns = jnp.floor(product * (1.0 / NLON) + 0.5)
            phase = product - turns * NLON
            size = jnp.abs(phase)
            cosine = quarter_sine((640.0 - size) * (1.0 / 640.0))
            fold = 640.0 - jnp.abs(size - 640.0)
            sine = quarter_sine(jnp.where(phase < 0, fold, -fold) * (1.0 / 640.0))
            pair = jnp.concatenate(
                [cosine.reshape(8, 8, 128), sine.reshape(8, 8, 128)], axis=1
            ).reshape(128, 128)
            trig[pl.ds(pl.multiple_of(b * 128, 128), 128), t * 128:(t + 1) * 128] = (
                pair.astype(BF16)
            )

    leg_copy.wait()
    for r in range(2):
        @pl.loop(0, 10)
        def _(s):
            rows = pl.ds(pl.multiple_of(s * 128, 128), 128)
            for u in range(5):
                leg32[u, rows, :] = leg_v[r, rows, u * 128:(u + 1) * 128].astype(F32)

        @pl.loop(0, 8)
        def _(j):
            for i in range(5):
                for u in range(5):
                    rows = pl.ds(pl.multiple_of(i * 256 + j * 32, 32), 32)
                    legp[r, rows, u * 128:(u + 1) * 128] = leg32[
                        u, pl.ds(j * 5 + i, 32, stride=40), :
                    ].astype(BF16)

    def fields_of(shape, axis):
        row = lax.broadcasted_iota(jnp.int32, shape, axis).astype(F32)
        group = jnp.floor((row + 0.5) * (1.0 / 32.0))
        within = row - 32.0 * group
        field = float(FG) * group + within
        vector = jnp.floor((field + 0.5) * (1.0 / 3.0))
        return within < FG - 0.5, vector, field - 3.0 * vector

    used, _, level = fields_of((192, NT), 0)
    wts[...] = jnp.where(
        used,
        jnp.where(
            level < 0.5,
            ew_ref[0:1, :],
            jnp.where(level < 1.5, ew_ref[1:2, :], ew_ref[2:3, :]),
        ),
        0.0,
    )

    def analyse(c):
        first, count = CHUNKS[c]
        window = xa.at[pl.ds(first * 128, count * 128), pl.ds(0, 1792)]
        pltpu.make_async_copy(window, window, s1_recv.at[c]).wait()
        window = xrr.at[pl.ds(0, 7), pl.ds(first * 64, count * 64)]
        pltpu.make_async_copy(window, window, s1r_recv.at[c]).wait()
        own_copy(c).wait()
        for g in range(first, first + count):
            for m in range(4):
                even = xrr[2 * m, g * 64:(g + 1) * 64, :].astype(F32)
                odd = xrr[2 * m + 1, g * 64:(g + 1) * 64, :].astype(F32)
                cols = slice(2048 + m * 128, 2176 + m * 128)
                xa[g * 128:g * 128 + 64, cols] = jnp.where(
                    low, even, pltpu.roll(odd, 64, 1)
                ).astype(BF16)
                xa[g * 128 + 64:g * 128 + 128, cols] = jnp.where(
                    low, pltpu.roll(even, 64, 1), odd
                ).astype(BF16)

        @pl.loop(0, 2)
        def _(h):
            half = lax.rem(lat // 16 + 1 + h, 2)
            rows = pl.ds(pl.multiple_of(half * 512, 512), 512)
            product = nt_dot(trig[rows, :], xa[first * 128:(first + count) * 128, :])
            product = (product * (1.0 / math.sqrt(NLON))).astype(BF16)
            for g in range(count):
                sb[first + g, pl.ds(half * 16, 16)] = product[
                    :, g * 128:(g + 1) * 128
                ].reshape(16, 32, 128)

            @pl.loop(0, 16)
            def _(k):
                peer = half * 16 + lax.rem(lat + k + 8, 16)

                @pl.when(peer != lat)
                def _():
                    pltpu.make_async_remote_copy(
                        src_ref=sb.at[pl.ds(first, count), peer],
                        dst_ref=zb.at[pl.ds(first, count), lat],
                        send_sem=zy_send, recv_sem=zy_recv.at[c],
                        device_id=(peer, lon), device_id_type=MESH,
                    ).start()

        for g in range(first, first + count):
            zb[g, lat] = sb[g, lat]

    def deliver(c):
        first, count = CHUNKS[c]
        window = sb.at[pl.ds(first, count), pl.ds(0, 31)]
        pltpu.make_async_copy(window, window, zy_recv.at[c]).wait()
        for g in range(first, first + count):
            @pl.loop(0, 8)
            def _(s):
                for e in range(4):
                    rows = zb[g, s * 4 + e].astype(F32)
                    for rp in range(4):
                        r32[pl.ds(s * 16 + e * 4 + rp, 8, stride=136), :] = rows[
                            rp * 8:(rp + 1) * 8
                        ]

            for j in range(8):
                rbs[g, j] = r32[j * 136:j * 136 + 128, :].astype(BF16)

        @pl.loop(1, 8)
        def _(k):
            peer = lax.rem(lon + k, 8)
            pltpu.make_async_remote_copy(
                src_ref=rbs.at[pl.ds(first, count), peer],
                dst_ref=rb.at[pl.ds(first, count), lon],
                send_sem=s2_send, recv_sem=s2_recv.at[c],
                device_id=(lat, peer), device_id_type=MESH,
            ).start()

        for g in range(first, first + count):
            rb[g, lon] = rbs[g, lon]

    slot = (lat * 8 + lon) * 2

    def collect(c):
        first, count = CHUNKS[c]
        window = rb.at[pl.ds(first, count), pl.ds(0, 7)]
        pltpu.make_async_copy(window, window, s2_recv.at[c]).wait()
        for g in range(first, first + count):
            @pl.loop(0, 8)
            def _(j):
                c32[pl.ds(pl.multiple_of(j * 128, 128), 128), :] = rb[g, j].astype(F32)

            for r in range(2):
                for p in range(2):
                    ext32[0:128, :] = jnp.transpose(c32[pl.ds(r * 2 + p, 256, stride=4), :])
                    for i in range(5):
                        amat[r, p, g * 32:(g + 1) * 32, i * 256:(i + 1) * 256] = ext32[
                            FG * i:FG * i + 32, :
                        ].astype(BF16)
        rows = slice(first * 32, (first + count) * 32)
        degree = lax.broadcasted_iota(jnp.int32, (count * 64, NT), 1)
        for r in range(2):
            full = jnp.dot(
                amat[r, :, rows, :].reshape(count * 64, 1280), legp[r],
                preferred_element_type=F32,
            )
            full = jnp.where(degree >= wave_ref[slot + r], full, 0.0)
            for p in range(2):
                part = full[p * count * 32:(p + 1) * count * 32]
                out[r, p, rows, :] = part
                for g in range(count):
                    start = 4 * FG * (first + g) + r * 2 + p
                    for u in range(5):
                        ost[u, pl.ds(start, 32, stride=4), :] = part[
                            g * 32:(g + 1) * 32, u * 128:(u + 1) * 128
                        ]

    analyse(0)
    analyse(1)
    analyse(2)
    analyse(3)
    deliver(0)
    deliver(1)
    analyse(4)
    collect(0)
    deliver(2)
    collect(1)
    deliver(3)
    collect(2)
    deliver(4)
    collect(3)
    collect(4)

    total = jnp.zeros((192, 192), F32)
    for r in range(2):
        factor = jnp.where(wave_ref[slot + r] == 0, 1.0, 2.0).astype(F32)
        for p in range(2):
            part = out[r, p]
            total += nt_dot(part.astype(BF16), (part * (wts[...] * factor)).astype(BF16))

    _, _, row_level = fields_of((192, 192), 0)
    _, _, col_level = fields_of((192, 192), 1)
    total = jnp.where(row_level == col_level, total, 0.0)
    vec = lax.broadcasted_iota(jnp.int32, (128, 192), 0).astype(F32)
    used, vector, _ = fields_of((128, 192), 1)
    pick = jnp.where(used & (vector == vec), 1.0, 0.0).astype(F32)
    upper = jnp.where(used & (vector == vec - 64.0), 1.0, 0.0).astype(F32)
    high = lax.Precision.HIGHEST
    half = jnp.dot(pick[0:64], total, preferred_element_type=F32, precision=high)
    packed = nt_dot(half[0:32], pick, high) + nt_dot(half[32:64], upper, high)
    gs[...] = (packed * (1.0 / (LEV * M * NT))).reshape(8, 4, 128)

    def ring(which, src, dst):
        @pl.loop(1, 8)
        def _(k):
            peer = lax.rem(lon + k, 8)
            pltpu.make_async_remote_copy(
                src_ref=src(peer), dst_ref=dst.at[lon],
                send_sem=g_send.at[which], recv_sem=g_recv.at[which],
                device_id=(lat, peer), device_id_type=MESH,
            ).start()

    ring(0, lambda peer: gs.at[peer], ga)
    ga[lon] = gs[lon]
    for u in range(5):
        spec_v[:, :, u * 128:(u + 1) * 128] = ost[u, 0:600, :].reshape(300, 2, 128).astype(BF16)
    store = pltpu.make_async_copy(spec_v, spec_ref, spec_sem)
    store.start()
    pltpu.make_async_copy(ga.at[pl.ds(0, 7)], ga.at[pl.ds(0, 7)], g_recv.at[0]).wait()
    gb[lat] = jnp.sum(ga[...], axis=0)

    @pl.loop(1, 32)
    def _(k):
        peer = lax.rem(lat + 1 + lax.rem(k + 11, 31), 32)
        pltpu.make_async_remote_copy(
            src_ref=gb.at[lat], dst_ref=gb.at[lat],
            send_sem=g_send.at[1], recv_sem=g_recv.at[1],
            device_id=(peer, lon), device_id_type=MESH,
        ).start()

    pltpu.make_async_copy(gb.at[pl.ds(0, 31)], gb.at[pl.ds(0, 31)], g_recv.at[1]).wait()
    gc[lon] = jnp.sum(gb[...], axis=0)
    ring(2, lambda peer: gc.at[lon], gc)
    pltpu.make_async_copy(gc.at[pl.ds(0, 7)], gc.at[pl.ds(0, 7)], g_recv.at[2]).wait()
    packed = gc[...].reshape(32, 128)
    gram_ref[0:32, :] = packed[:, 0:50]
    gram_ref[32:50, :] = packed[0:18, 64:114]

    store.wait()

    window = xa.at[:, pl.ds(0, 1792)]
    pltpu.make_async_copy(window, window, s1_send).wait()
    window = xrr.at[pl.ds(0, 7)]
    pltpu.make_async_copy(window, window, s1r_send).wait()
    window = sb.at[:, pl.ds(0, 31)]
    pltpu.make_async_copy(window, window, zy_send).wait()
    window = rb.at[:, pl.ds(0, 7)]
    pltpu.make_async_copy(window, window, s2_send).wait()
    pltpu.make_async_copy(ga.at[pl.ds(0, 7)], ga.at[pl.ds(0, 7)], g_send.at[0]).wait()
    pltpu.make_async_copy(gb.at[pl.ds(0, 31)], gb.at[pl.ds(0, 31)], g_send.at[1]).wait()
    pltpu.make_async_copy(gc.at[pl.ds(0, 7)], gc.at[pl.ds(0, 7)], g_send.at[2]).wait()


def hand_on(spec_in, gram_in, spec_out, gram_out, sems):
    copies = [
        pltpu.make_async_copy(gram_in, gram_out, sems.at[3]),
    ] + [
        pltpu.make_async_copy(
            spec_in.at[pl.ds(100 * b, 100)], spec_out.at[pl.ds(100 * b, 100)], sems.at[b]
        )
        for b in range(3)
    ]
    for copy in copies:
        copy.start()
    for copy in copies:
        copy.wait()


def on_device(grid_fields, legendre, wave_of_slot, energy_weight):
    rows = grid_fields.transpose(1, 2, 0, 3).reshape(150, 40, 320)
    waves = wave_of_slot.reshape(4, 128)
    vmem = pl.BlockSpec(memory_space=pltpu.VMEM)
    dma = pltpu.SemaphoreType.DMA
    many = dma((len(CHUNKS),))
    spectral, gram_matrix = pl.pallas_call(
        kernel,
        out_shape=(
            jax.ShapeDtypeStruct((300, 2, NT), BF16),
            jax.ShapeDtypeStruct((50, 50), F32),
        ),
        in_specs=[
            pl.BlockSpec(memory_space=pl.ANY),
            pl.BlockSpec(memory_space=pl.ANY),
            vmem,
            pl.BlockSpec(memory_space=pltpu.SMEM),
            vmem,
        ],
        out_specs=(pl.BlockSpec(memory_space=pl.ANY), vmem),
        scratch_shapes=[
            pltpu.VMEM((150, 40, 320), BF16),
            pltpu.VMEM((6, 3, 1008, 128), F32),
            pltpu.VMEM((8, 768, 256), BF16),
            pltpu.VMEM((8, 384, 128), BF16),
            pltpu.VMEM((768, NLON), BF16),
            pltpu.VMEM((8, 384, 128), BF16),
            pltpu.VMEM((1024, NLON), BF16),
            pltpu.VMEM((512, 128), F32),
            pltpu.VMEM((512, 128), F32),
            pltpu.VMEM((6, 32, 32, 128), BF16),
            pltpu.VMEM((6, 32, 32, 128), BF16),
            pltpu.VMEM((8 * 136, 128), F32),
            pltpu.VMEM((6, 8, 128, 128), BF16),
            pltpu.VMEM((6, 8, 128, 128), BF16),
            pltpu.VMEM((2, 1280, NT), BF16),
            pltpu.VMEM((5, 1280, 128), F32),
            pltpu.VMEM((2, 1280, NT), BF16),
            pltpu.VMEM((1024, 128), F32),
            pltpu.VMEM((136, 256), F32),
            pltpu.VMEM((2, 2, 192, 1280), BF16),
            pltpu.VMEM((2, 2, 192, NT), F32),
            pltpu.VMEM((5, 632, 128), F32),
            pltpu.VMEM((192, NT), F32),
            pltpu.VMEM((300, 2, NT), BF16),
            pltpu.VMEM((8, 4, 128), F32),
            pltpu.VMEM((8, 4, 128), F32),
            pltpu.VMEM((32, 4, 128), F32),
            pltpu.VMEM((8, 4, 128), F32),
            dma((6,)), dma, dma, many, dma, many, dma, many,
            dma, many, dma, many, dma((3,)), dma((3,)),
        ],
        compiler_params=pltpu.CompilerParams(
            collective_id=0, has_side_effects=True, vmem_limit_bytes=60 * 1024 * 1024,
        ),
        cost_estimate=pl.CostEstimate(
            flops=6_000_000_000, bytes_accessed=12_000_000, transcendentals=0
        ),
    )(rows, legendre, waves, wave_of_slot, energy_weight)
    anywhere = pl.BlockSpec(memory_space=pl.ANY)
    spectral, gram_matrix = pl.pallas_call(
        hand_on,
        out_shape=(
            jax.ShapeDtypeStruct((300, 2, NT), BF16),
            jax.ShapeDtypeStruct((50, 50), F32),
        ),
        in_specs=[vmem, vmem],
        out_specs=(anywhere, anywhere),
        scratch_shapes=[dma((4,))],
    )(spectral, gram_matrix)
    return spectral.reshape(50, LEV, 2, 2, NT), gram_matrix


def solution(mesh):
    placed = (P("lat", None, None, "lon"), P(("lat", "lon"), None, None), P(), P())
    return jax.shard_map(
        on_device,
        mesh=mesh,
        in_specs=placed,
        out_specs=(P(None, None, ("lat", "lon"), None, None), P()),
        check_vma=False,
    )
```

```python
import math

import jax
import jax.numpy as jnp
from jax import lax
from jax.experimental import pallas as pl
from jax.experimental.pallas import tpu as pltpu
from jax.sharding import PartitionSpec as P

NLON = 2560
M = 512
NT = 640
LEV = 3
F32 = jnp.float32
BF16 = jnp.bfloat16
MESH = pl.DeviceIdType.MESH

FG = 25
CHUNKS = tuple((g, 1) for g in range(6))
SIN_COEF = tuple(
    (-1) ** i * (math.pi / 2) ** (2 * i + 1) / math.factorial(2 * i + 1) for i in range(6)
)


def quarter_sine(z):
    square = z * z
    total = jnp.full_like(z, SIN_COEF[5])
    for coef in SIN_COEF[4::-1]:
        total = total * square + coef
    return total * z


def nt_dot(a, b, precision=None):
    return lax.dot_general(
        a, b, (((1,), (1,)), ((), ())), preferred_element_type=F32, precision=precision
    )


def kernel(
    x_hbm, leg_hbm, wq_ref, wave_ref, ew_ref, spec_ref, gram_ref,
    xv, x32, xs, xrs, xa, xrr, trig, wn, w32, sb, zb, r32, rbs, rb, leg_v, leg32, legp,
    c32, ext32, amat, out, ost, wts, spec_v, gs, ga, gb, gc,
    x_sem, leg_sem, spec_sem, own_sem, s1_send, s1_recv, s1r_send, s1r_recv,
    zy_send, zy_recv, s2_send, s2_recv, g_send, g_recv,
):
    lat = lax.axis_index("lat")
    lon = lax.axis_index("lon")

    def load_x(g):
        rows = pl.ds(FG * g, FG)
        return pltpu.make_async_copy(x_hbm.at[rows], xv.at[rows], x_sem.at[g])

    for g in range(6):
        load_x(g).start()
    leg_copy = pltpu.make_async_copy(leg_hbm, leg_v, leg_sem)
    leg_copy.start()

    barrier = pltpu.get_barrier_semaphore()

    @pl.loop(1, 8)
    def _(k):
        pl.semaphore_signal(
            barrier, inc=1, device_id=(lat, lax.rem(lon + k, 8)), device_id_type=MESH
        )

    @pl.loop(1, 32)
    def _(k):
        pl.semaphore_signal(
            barrier, inc=1, device_id=(lax.rem(lat + k, 32), lon), device_id_type=MESH
        )

    x32[:, :, 1000:1008, :] = jnp.zeros((6, 3, 8, 128), F32)
    ext32[128:136, :] = jnp.zeros((8, 256), F32)

    def relay(g):
        load_x(g).wait()

        @pl.loop(0, FG)
        def _(u):
            rows = xv[FG * g + u].astype(F32)
            for t in range(3):
                width = 128 if t < 2 else 64
                x32[g, t, pl.ds(u, 40, stride=FG), 0:width] = rows[
                    :, t * 128:t * 128 + width
                ]

    def main_copy(c, peer):
        first, count = CHUNKS[c]
        rows = pl.ds(first * 128, count * 128)
        return pltpu.make_async_remote_copy(
            src_ref=xs.at[peer, rows],
            dst_ref=xa.at[rows, pl.ds(pl.multiple_of(lon * 256, 256), 256)],
            send_sem=s1_send, recv_sem=s1_recv.at[c],
            device_id=(lat, peer), device_id_type=MESH,
        )

    def rest_copy(c, peer):
        first, count = CHUNKS[c]
        rows = pl.ds(first * 64, count * 64)
        return pltpu.make_async_remote_copy(
            src_ref=xrs.at[peer, rows], dst_ref=xrr.at[lon, rows],
            send_sem=s1r_send, recv_sem=s1r_recv.at[c],
            device_id=(lat, peer), device_id_type=MESH,
        )

    low = lax.broadcasted_iota(jnp.int32, (64, 128), 1) < 64

    def pack(c, peer):
        first, count = CHUNKS[c]
        for g in range(first, first + count):
            for t in range(2):
                xs[peer, g * 128:(g + 1) * 128, t * 128:(t + 1) * 128] = x32[
                    g, t, pl.ds(peer * 125, 128), :
                ].astype(BF16)
            rest = x32[g, 2, pl.ds(peer * 125, 128), :]
            rest = jnp.where(low, rest[0:64], pltpu.roll(rest[64:128], 64, 1))
            xrs[peer, g * 64:(g + 1) * 64, :] = rest.astype(BF16)

    def own_copy(c):
        first, count = CHUNKS[c]
        rows = pl.ds(first * 128, count * 128)
        return pltpu.make_async_copy(
            xs.at[lon, rows],
            xa.at[rows, pl.ds(pl.multiple_of(lon * 256, 256), 256)],
            own_sem.at[c],
        )

    for c, (first, count) in enumerate(CHUNKS):
        for g in range(first, first + count):
            relay(g)
        if c == 0:
            pl.semaphore_wait(barrier, 38)

        @pl.loop(1, 8)
        def _(k):
            peer = lax.rem(lon + k, 8)
            pack(c, peer)
            main_copy(c, peer).start()
            rest_copy(c, peer).start()

    for c, (first, count) in enumerate(CHUNKS):
        pack(c, lon)
        own_copy(c).start()
        for g in range(first, first + count):
            xrr[lon, g * 64:(g + 1) * 64, :] = xrs[lon, g * 64:(g + 1) * 64, :]

    lane = lax.broadcasted_iota(jnp.int32, (1, 128), 1)
    for b in range(4):
        wn[b * 128:(b + 1) * 128, :] = jnp.transpose(
            jnp.broadcast_to(wq_ref[b:b + 1, :].astype(F32), (128, 128))
        )

    @pl.loop(0, 32)
    def _(z):
        for r in range(2):
            w32[pl.ds(pl.multiple_of(z * 16 + r * 8, 8), 8), :] = wn[
                pl.ds(z * 16 + r, 8, stride=2), :
            ]

    @pl.loop(0, 8)
    def _(b):
        waves = w32[pl.ds(pl.multiple_of(b * 64, 64), 64), :]
        for t in range(20):
            if t < 16:
                place = lane + ((t // 2) * 320 + (t % 2) * 128)
            else:
                m = t - 16
                place = jnp.where(lane < 64, lane + (640 * m + 256), lane + (640 * m + 512))
            product = waves * place.astype(F32)
            turns = jnp.floor(product * (1.0 / NLON) + 0.5)
            phase = product - turns * NLON
            size = jnp.abs(phase)
            cosine = quarter_sine((640.0 - size) * (1.0 / 640.0))
            fold = 640.0 - jnp.abs(size - 640.0)
            sine = quarter_sine(jnp.where(phase < 0, fold, -fold) * (1.0 / 640.0))
            pair = jnp.concatenate(
                [cosine.reshape(8, 8, 128), sine.reshape(8, 8, 128)], axis=1
            ).reshape(128, 128)
            trig[pl.ds(pl.multiple_of(b * 128, 128), 128), t * 128:(t + 1) * 128] = (
                pair.astype(BF16)
            )

    leg_copy.wait()
    for r in range(2):
        @pl.loop(0, 10)
        def _(s):
            rows = pl.ds(pl.multiple_of(s * 128, 128), 128)
            for u in range(5):
                leg32[u, rows, :] = leg_v[r, rows, u * 128:(u + 1) * 128].astype(F32)

        @pl.loop(0, 8)
        def _(j):
            for i in range(5):
                for u in range(5):
                    rows = pl.ds(pl.multiple_of(i * 256 + j * 32, 32), 32)
                    legp[r, rows, u * 128:(u + 1) * 128] = leg32[
                        u, pl.ds(j * 5 + i, 32, stride=40), :
                    ].astype(BF16)

    def fields_of(shape, axis):
        row = lax.broadcasted_iota(jnp.int32, shape, axis).astype(F32)
        group = jnp.floor((row + 0.5) * (1.0 / 32.0))
        within = row - 32.0 * group
        field = float(FG) * group + within
        vector = jnp.floor((field + 0.5) * (1.0 / 3.0))
        return within < FG - 0.5, vector, field - 3.0 * vector

    used, _, level = fields_of((192, NT), 0)
    wts[...] = jnp.where(
        used,
        jnp.where(
            level < 0.5,
            ew_ref[0:1, :],
            jnp.where(level < 1.5, ew_ref[1:2, :], ew_ref[2:3, :]),
        ),
        0.0,
    )

    def analyse(c):
        first, count = CHUNKS[c]
        window = xa.at[pl.ds(first * 128, count * 128), pl.ds(0, 1792)]
        pltpu.make_async_copy(window, window, s1_recv.at[c]).wait()
        window = xrr.at[pl.ds(0, 7), pl.ds(first * 64, count * 64)]
        pltpu.make_async_copy(window, window, s1r_recv.at[c]).wait()
        own_copy(c).wait()
        for g in range(first, first + count):
            for m in range(4):
                even = xrr[2 * m, g * 64:(g + 1) * 64, :].astype(F32)
                odd = xrr[2 * m + 1, g * 64:(g + 1) * 64, :].astype(F32)
                cols = slice(2048 + m * 128, 2176 + m * 128)
                xa[g * 128:g * 128 + 64, cols] = jnp.where(
                    low, even, pltpu.roll(odd, 64, 1)
                ).astype(BF16)
                xa[g * 128 + 64:g * 128 + 128, cols] = jnp.where(
                    low, pltpu.roll(even, 64, 1), odd
                ).astype(BF16)

        @pl.loop(0, 2)
        def _(h):
            half = lax.rem(lat // 16 + 1 + h, 2)
            rows = pl.ds(pl.multiple_of(half * 512, 512), 512)
            product = nt_dot(trig[rows, :], xa[first * 128:(first + count) * 128, :])
            product = (product * (1.0 / math.sqrt(NLON))).astype(BF16)
            for g in range(count):
                sb[first + g, pl.ds(half * 16, 16)] = product[
                    :, g * 128:(g + 1) * 128
                ].reshape(16, 32, 128)

            @pl.loop(0, 16)
            def _(k):
                peer = half * 16 + lax.rem(lat + k + 8, 16)

                @pl.when(peer != lat)
                def _():
                    pltpu.make_async_remote_copy(
                        src_ref=sb.at[pl.ds(first, count), peer],
                        dst_ref=zb.at[pl.ds(first, count), lat],
                        send_sem=zy_send, recv_sem=zy_recv.at[c],
                        device_id=(peer, lon), device_id_type=MESH,
                    ).start()

        for g in range(first, first + count):
            zb[g, lat] = sb[g, lat]

    def deliver(c):
        first, count = CHUNKS[c]
        window = sb.at[pl.ds(first, count), pl.ds(0, 31)]
        pltpu.make_async_copy(window, window, zy_recv.at[c]).wait()
        for g in range(first, first + count):
            @pl.loop(0, 8)
            def _(s):
                for e in range(4):
                    rows = zb[g, s * 4 + e].astype(F32)
                    for rp in range(4):
                        r32[pl.ds(s * 16 + e * 4 + rp, 8, stride=136), :] = rows[
                            rp * 8:(rp + 1) * 8
                        ]

            for j in range(8):
                rbs[g, j] = r32[j * 136:j * 136 + 128, :].astype(BF16)

        @pl.loop(1, 8)
        def _(k):
            peer = lax.rem(lon + k, 8)
            pltpu.make_async_remote_copy(
                src_ref=rbs.at[pl.ds(first, count), peer],
                dst_ref=rb.at[pl.ds(first, count), lon],
                send_sem=s2_send, recv_sem=s2_recv.at[c],
                device_id=(lat, peer), device_id_type=MESH,
            ).start()

        for g in range(first, first + count):
            rb[g, lon] = rbs[g, lon]

    slot = (lat * 8 + lon) * 2

    def collect(c):
        first, count = CHUNKS[c]
        window = rb.at[pl.ds(first, count), pl.ds(0, 7)]
        pltpu.make_async_copy(window, window, s2_recv.at[c]).wait()
        for g in range(first, first + count):
            @pl.loop(0, 8)
            def _(j):
                c32[pl.ds(pl.multiple_of(j * 128, 128), 128), :] = rb[g, j].astype(F32)

            for r in range(2):
                for p in range(2):
                    ext32[0:128, :] = jnp.transpose(c32[pl.ds(r * 2 + p, 256, stride=4), :])
                    for i in range(5):
                        amat[r, p, g * 32:(g + 1) * 32, i * 256:(i + 1) * 256] = ext32[
                            FG * i:FG * i + 32, :
                        ].astype(BF16)
        rows = slice(first * 32, (first + count) * 32)
        degree = lax.broadcasted_iota(jnp.int32, (count * 64, NT), 1)
        for r in range(2):
            full = jnp.dot(
                amat[r, :, rows, :].reshape(count * 64, 1280), legp[r],
                preferred_element_type=F32,
            )
            full = jnp.where(degree >= wave_ref[slot + r], full, 0.0)
            for p in range(2):
                part = full[p * count * 32:(p + 1) * count * 32]
                out[r, p, rows, :] = part
                for g in range(count):
                    start = 4 * FG * (first + g) + r * 2 + p
                    for u in range(5):
                        ost[u, pl.ds(start, 32, stride=4), :] = part[
                            g * 32:(g + 1) * 32, u * 128:(u + 1) * 128
                        ]

    analyse(0)
    analyse(1)
    analyse(2)
    analyse(3)
    deliver(0)
    analyse(4)
    deliver(1)
    deliver(2)
    analyse(5)
    deliver(3)
    collect(0)
    deliver(4)
    collect(1)
    collect(2)
    deliver(5)
    collect(3)
    collect(4)
    collect(5)

    total = jnp.zeros((192, 192), F32)
    for r in range(2):
        factor = jnp.where(wave_ref[slot + r] == 0, 1.0, 2.0).astype(F32)
        for p in range(2):
            part = out[r, p]
            total += nt_dot(part.astype(BF16), (part * (wts[...] * factor)).astype(BF16))

    _, _, row_level = fields_of((192, 192), 0)
    _, _, col_level = fields_of((192, 192), 1)
    total = jnp.where(row_level == col_level, total, 0.0)
    vec = lax.broadcasted_iota(jnp.int32, (128, 192), 0).astype(F32)
    used, vector, _ = fields_of((128, 192), 1)
    pick = jnp.where(used & (vector == vec), 1.0, 0.0).astype(F32)
    upper = jnp.where(used & (vector == vec - 64.0), 1.0, 0.0).astype(F32)
    high = lax.Precision.HIGHEST
    half = jnp.dot(pick[0:64], total, preferred_element_type=F32, precision=high)
    packed = nt_dot(half[0:32], pick, high) + nt_dot(half[32:64], upper, high)
    gs[...] = (packed * (1.0 / (LEV * M * NT))).reshape(8, 4, 128)

    def ring(which, src, dst):
        @pl.loop(1, 8)
        def _(k):
            peer = lax.rem(lon + k, 8)
            pltpu.make_async_remote_copy(
                src_ref=src(peer), dst_ref=dst.at[lon],
                send_sem=g_send.at[which], recv_sem=g_recv.at[which],
                device_id=(lat, peer), device_id_type=MESH,
            ).start()

    ring(0, lambda peer: gs.at[peer], ga)
    ga[lon] = gs[lon]
    for u in range(5):
        spec_v[:, :, u * 128:(u + 1) * 128] = ost[u, 0:600, :].reshape(300, 2, 128).astype(BF16)
    store = pltpu.make_async_copy(spec_v, spec_ref, spec_sem)
    store.start()
    pltpu.make_async_copy(ga.at[pl.ds(0, 7)], ga.at[pl.ds(0, 7)], g_recv.at[0]).wait()
    gb[lat] = jnp.sum(ga[...], axis=0)

    @pl.loop(1, 32)
    def _(k):
        peer = lax.rem(lat + 1 + lax.rem(k + 11, 31), 32)
        pltpu.make_async_remote_copy(
            src_ref=gb.at[lat], dst_ref=gb.at[lat],
            send_sem=g_send.at[1], recv_sem=g_recv.at[1],
            device_id=(peer, lon), device_id_type=MESH,
        ).start()

    pltpu.make_async_copy(gb.at[pl.ds(0, 31)], gb.at[pl.ds(0, 31)], g_recv.at[1]).wait()
    gc[lon] = jnp.sum(gb[...], axis=0)
    ring(2, lambda peer: gc.at[lon], gc)
    pltpu.make_async_copy(gc.at[pl.ds(0, 7)], gc.at[pl.ds(0, 7)], g_recv.at[2]).wait()
    packed = gc[...].reshape(32, 128)
    gram_ref[0:32, :] = packed[:, 0:50]
    gram_ref[32:50, :] = packed[0:18, 64:114]

    store.wait()

    window = xa.at[:, pl.ds(0, 1792)]
    pltpu.make_async_copy(window, window, s1_send).wait()
    window = xrr.at[pl.ds(0, 7)]
    pltpu.make_async_copy(window, window, s1r_send).wait()
    window = sb.at[:, pl.ds(0, 31)]
    pltpu.make_async_copy(window, window, zy_send).wait()
    window = rb.at[:, pl.ds(0, 7)]
    pltpu.make_async_copy(window, window, s2_send).wait()
    pltpu.make_async_copy(ga.at[pl.ds(0, 7)], ga.at[pl.ds(0, 7)], g_send.at[0]).wait()
    pltpu.make_async_copy(gb.at[pl.ds(0, 31)], gb.at[pl.ds(0, 31)], g_send.at[1]).wait()
    pltpu.make_async_copy(gc.at[pl.ds(0, 7)], gc.at[pl.ds(0, 7)], g_send.at[2]).wait()


def hand_on(spec_in, gram_in, spec_out, gram_out, sems):
    copies = [
        pltpu.make_async_copy(gram_in, gram_out, sems.at[3]),
    ] + [
        pltpu.make_async_copy(
            spec_in.at[pl.ds(100 * b, 100)], spec_out.at[pl.ds(100 * b, 100)], sems.at[b]
        )
        for b in range(3)
    ]
    for copy in copies:
        copy.start()
    for copy in copies:
        copy.wait()


def on_device(grid_fields, legendre, wave_of_slot, energy_weight):
    rows = grid_fields.transpose(1, 2, 0, 3).reshape(150, 40, 320)
    waves = wave_of_slot.reshape(4, 128)
    vmem = pl.BlockSpec(memory_space=pltpu.VMEM)
    dma = pltpu.SemaphoreType.DMA
    many = dma((len(CHUNKS),))
    spectral, gram_matrix = pl.pallas_call(
        kernel,
        out_shape=(
            jax.ShapeDtypeStruct((300, 2, NT), BF16),
            jax.ShapeDtypeStruct((50, 50), F32),
        ),
        in_specs=[
            pl.BlockSpec(memory_space=pl.ANY),
            pl.BlockSpec(memory_space=pl.ANY),
            vmem,
            pl.BlockSpec(memory_space=pltpu.SMEM),
            vmem,
        ],
        out_specs=(pl.BlockSpec(memory_space=pl.ANY), vmem),
        scratch_shapes=[
            pltpu.VMEM((150, 40, 320), BF16),
            pltpu.VMEM((6, 3, 1008, 128), F32),
            pltpu.VMEM((8, 768, 256), BF16),
            pltpu.VMEM((8, 384, 128), BF16),
            pltpu.VMEM((768, NLON), BF16),
            pltpu.VMEM((8, 384, 128), BF16),
            pltpu.VMEM((1024, NLON), BF16),
            pltpu.VMEM((512, 128), F32),
            pltpu.VMEM((512, 128), F32),
            pltpu.VMEM((6, 32, 32, 128), BF16),
            pltpu.VMEM((6, 32, 32, 128), BF16),
            pltpu.VMEM((8 * 136, 128), F32),
            pltpu.VMEM((6, 8, 128, 128), BF16),
            pltpu.VMEM((6, 8, 128, 128), BF16),
            pltpu.VMEM((2, 1280, NT), BF16),
            pltpu.VMEM((5, 1280, 128), F32),
            pltpu.VMEM((2, 1280, NT), BF16),
            pltpu.VMEM((1024, 128), F32),
            pltpu.VMEM((136, 256), F32),
            pltpu.VMEM((2, 2, 192, 1280), BF16),
            pltpu.VMEM((2, 2, 192, NT), F32),
            pltpu.VMEM((5, 632, 128), F32),
            pltpu.VMEM((192, NT), F32),
            pltpu.VMEM((300, 2, NT), BF16),
            pltpu.VMEM((8, 4, 128), F32),
            pltpu.VMEM((8, 4, 128), F32),
            pltpu.VMEM((32, 4, 128), F32),
            pltpu.VMEM((8, 4, 128), F32),
            dma((6,)), dma, dma, many, dma, many, dma, many,
            dma, many, dma, many, dma((3,)), dma((3,)),
        ],
        compiler_params=pltpu.CompilerParams(
            collective_id=0, has_side_effects=True, vmem_limit_bytes=60 * 1024 * 1024,
        ),
        cost_estimate=pl.CostEstimate(
            flops=6_000_000_000, bytes_accessed=12_000_000, transcendentals=0
        ),
    )(rows, legendre, waves, wave_of_slot, energy_weight)
    anywhere = pl.BlockSpec(memory_space=pl.ANY)
    spectral, gram_matrix = pl.pallas_call(
        hand_on,
        out_shape=(
            jax.ShapeDtypeStruct((300, 2, NT), BF16),
            jax.ShapeDtypeStruct((50, 50), F32),
        ),
        in_specs=[vmem, vmem],
        out_specs=(anywhere, anywhere),
        scratch_shapes=[dma((4,))],
    )(spectral, gram_matrix)
    return spectral.reshape(50, LEV, 2, 2, NT), gram_matrix


def solution(mesh):
    placed = (P("lat", None, None, "lon"), P(("lat", "lon"), None, None), P(), P())
    return jax.shard_map(
        on_device,
        mesh=mesh,
        in_specs=placed,
        out_specs=(P(None, None, ("lat", "lon"), None, None), P()),
        check_vma=False,
    )
```

```python
import math

import jax
import jax.numpy as jnp
from jax import lax
from jax.experimental import pallas as pl
from jax.experimental.pallas import tpu as pltpu
from jax.sharding import PartitionSpec as P

NLON = 2560
M = 512
NT = 640
LEV = 3
F32 = jnp.float32
BF16 = jnp.bfloat16
MESH = pl.DeviceIdType.MESH

FG = 25
CHUNKS = tuple((g, 1) for g in range(6))
SIN_COEF = tuple(
    (-1) ** i * (math.pi / 2) ** (2 * i + 1) / math.factorial(2 * i + 1) for i in range(6)
)


def quarter_sine(z):
    square = z * z
    total = jnp.full_like(z, SIN_COEF[5])
    for coef in SIN_COEF[4::-1]:
        total = total * square + coef
    return total * z


def nt_dot(a, b, precision=None):
    return lax.dot_general(
        a, b, (((1,), (1,)), ((), ())), preferred_element_type=F32, precision=precision
    )


def kernel(
    x_hbm, leg_hbm, wq_ref, wave_ref, ew_ref, spec_ref, gram_ref,
    xv, x32, xs, xrs, xa, xrr, trig, wn, w32, sb, zb, r32, rbs, rb, leg_v, leg32, legp,
    c32, ext32, amat, out, ost, wts, same, picks, spec_v, gs, ga, gb, gc,
    x_sem, leg_sem, spec_sem, own_sem, s1_send, s1_recv, s1r_send, s1r_recv,
    zy_send, zy_recv, s2_send, s2_recv, g_send, g_recv,
):
    lat = lax.axis_index("lat")
    lon = lax.axis_index("lon")

    def load_x(g):
        rows = pl.ds(FG * g, FG)
        return pltpu.make_async_copy(x_hbm.at[rows], xv.at[rows], x_sem.at[g])

    for g in range(6):
        load_x(g).start()
    leg_copy = pltpu.make_async_copy(leg_hbm, leg_v, leg_sem)
    leg_copy.start()

    barrier = pltpu.get_barrier_semaphore()

    @pl.loop(1, 8)
    def _(k):
        pl.semaphore_signal(
            barrier, inc=1, device_id=(lat, lax.rem(lon + k, 8)), device_id_type=MESH
        )

    @pl.loop(1, 32)
    def _(k):
        pl.semaphore_signal(
            barrier, inc=1, device_id=(lax.rem(lat + k, 32), lon), device_id_type=MESH
        )

    x32[:, :, 1000:1008, :] = jnp.zeros((6, 3, 8, 128), F32)
    ext32[128:136, :] = jnp.zeros((8, 256), F32)

    def relay(g):
        load_x(g).wait()

        @pl.loop(0, FG)
        def _(u):
            rows = xv[FG * g + u].astype(F32)
            for t in range(3):
                width = 128 if t < 2 else 64
                x32[g, t, pl.ds(u, 40, stride=FG), 0:width] = rows[
                    :, t * 128:t * 128 + width
                ]

    def main_copy(c, peer):
        first, count = CHUNKS[c]
        rows = pl.ds(first * 128, count * 128)
        return pltpu.make_async_remote_copy(
            src_ref=xs.at[peer, rows],
            dst_ref=xa.at[rows, pl.ds(pl.multiple_of(lon * 256, 256), 256)],
            send_sem=s1_send, recv_sem=s1_recv.at[c],
            device_id=(lat, peer), device_id_type=MESH,
        )

    def rest_copy(c, peer):
        first, count = CHUNKS[c]
        rows = pl.ds(first * 64, count * 64)
        return pltpu.make_async_remote_copy(
            src_ref=xrs.at[peer, rows], dst_ref=xrr.at[lon, rows],
            send_sem=s1r_send, recv_sem=s1r_recv.at[c],
            device_id=(lat, peer), device_id_type=MESH,
        )

    low = lax.broadcasted_iota(jnp.int32, (64, 128), 1) < 64

    def pack(c, peer):
        first, count = CHUNKS[c]
        for g in range(first, first + count):
            for t in range(2):
                xs[peer, g * 128:(g + 1) * 128, t * 128:(t + 1) * 128] = x32[
                    g, t, pl.ds(peer * 125, 128), :
                ].astype(BF16)
            rest = x32[g, 2, pl.ds(peer * 125, 128), :]
            rest = jnp.where(low, rest[0:64], pltpu.roll(rest[64:128], 64, 1))
            xrs[peer, g * 64:(g + 1) * 64, :] = rest.astype(BF16)

    def own_copy(c):
        first, count = CHUNKS[c]
        rows = pl.ds(first * 128, count * 128)
        return pltpu.make_async_copy(
            xs.at[lon, rows],
            xa.at[rows, pl.ds(pl.multiple_of(lon * 256, 256), 256)],
            own_sem.at[c],
        )

    for c, (first, count) in enumerate(CHUNKS):
        for g in range(first, first + count):
            relay(g)
        if c == 0:
            pl.semaphore_wait(barrier, 38)

        @pl.loop(1, 8)
        def _(k):
            peer = lax.rem(lon + k, 8)
            pack(c, peer)
            main_copy(c, peer).start()
            rest_copy(c, peer).start()

    for c, (first, count) in enumerate(CHUNKS):
        pack(c, lon)
        own_copy(c).start()
        for g in range(first, first + count):
            xrr[lon, g * 64:(g + 1) * 64, :] = xrs[lon, g * 64:(g + 1) * 64, :]

    lane = lax.broadcasted_iota(jnp.int32, (1, 128), 1)
    for b in range(4):
        wn[b * 128:(b + 1) * 128, :] = jnp.transpose(
            jnp.broadcast_to(wq_ref[b:b + 1, :].astype(F32), (128, 128))
        )

    @pl.loop(0, 32)
    def _(z):
        for r in range(2):
            w32[pl.ds(pl.multiple_of(z * 16 + r * 8, 8), 8), :] = wn[
                pl.ds(z * 16 + r, 8, stride=2), :
            ]

    @pl.loop(0, 8)
    def _(b):
        waves = w32[pl.ds(pl.multiple_of(b * 64, 64), 64), :]
        for t in range(20):
            if t < 16:
                place = lane + ((t // 2) * 320 + (t % 2) * 128)
            else:
                m = t - 16
                place = jnp.where(lane < 64, lane + (640 * m + 256), lane + (640 * m + 512))
            product = waves * place.astype(F32)
            turns = jnp.floor(product * (1.0 / NLON) + 0.5)
            phase = product - turns * NLON
            size = jnp.abs(phase)
            cosine = quarter_sine((640.0 - size) * (1.0 / 640.0))
            fold = 640.0 - jnp.abs(size - 640.0)
            sine = quarter_sine(jnp.where(phase < 0, fold, -fold) * (1.0 / 640.0))
            pair = jnp.concatenate(
                [cosine.reshape(8, 8, 128), sine.reshape(8, 8, 128)], axis=1
            ).reshape(128, 128)
            trig[pl.ds(pl.multiple_of(b * 128, 128), 128), t * 128:(t + 1) * 128] = (
                pair.astype(BF16)
            )

    leg_copy.wait()
    for r in range(2):
        @pl.loop(0, 10)
        def _(s):
            rows = pl.ds(pl.multiple_of(s * 128, 128), 128)
            for u in range(5):
                leg32[u, rows, :] = leg_v[r, rows, u * 128:(u + 1) * 128].astype(F32)

        @pl.loop(0, 8)
        def _(j):
            for i in range(5):
                for u in range(5):
                    rows = pl.ds(pl.multiple_of(i * 256 + j * 32, 32), 32)
                    legp[r, rows, u * 128:(u + 1) * 128] = leg32[
                        u, pl.ds(j * 5 + i, 32, stride=40), :
                    ].astype(BF16)

    def fields_of(shape, axis):
        row = lax.broadcasted_iota(jnp.int32, shape, axis).astype(F32)
        group = jnp.floor((row + 0.5) * (1.0 / 32.0))
        within = row - 32.0 * group
        field = float(FG) * group + within
        vector = jnp.floor((field + 0.5) * (1.0 / 3.0))
        return within < FG - 0.5, vector, field - 3.0 * vector

    used, _, level = fields_of((192, NT), 0)
    wts[...] = jnp.where(
        used,
        jnp.where(
            level < 0.5,
            ew_ref[0:1, :],
            jnp.where(level < 1.5, ew_ref[1:2, :], ew_ref[2:3, :]),
        ),
        0.0,
    )

    _, _, row_level = fields_of((192, 192), 0)
    _, _, col_level = fields_of((192, 192), 1)
    same[...] = jnp.where(row_level == col_level, 1.0, 0.0)
    vec = lax.broadcasted_iota(jnp.int32, (128, 192), 0).astype(F32)
    used, vector, _ = fields_of((128, 192), 1)
    picks[0] = jnp.where(used & (vector == vec), 1.0, 0.0).astype(F32)
    picks[1] = jnp.where(used & (vector == vec - 64.0), 1.0, 0.0).astype(F32)

    def analyse(c):
        first, count = CHUNKS[c]
        window = xa.at[pl.ds(first * 128, count * 128), pl.ds(0, 1792)]
        pltpu.make_async_copy(window, window, s1_recv.at[c]).wait()
        window = xrr.at[pl.ds(0, 7), pl.ds(first * 64, count * 64)]
        pltpu.make_async_copy(window, window, s1r_recv.at[c]).wait()
        own_copy(c).wait()
        for g in range(first, first + count):
            for m in range(4):
                even = xrr[2 * m, g * 64:(g + 1) * 64, :].astype(F32)
                odd = xrr[2 * m + 1, g * 64:(g + 1) * 64, :].astype(F32)
                cols = slice(2048 + m * 128, 2176 + m * 128)
                xa[g * 128:g * 128 + 64, cols] = jnp.where(
                    low, even, pltpu.roll(odd, 64, 1)
                ).astype(BF16)
                xa[g * 128 + 64:g * 128 + 128, cols] = jnp.where(
                    low, pltpu.roll(even, 64, 1), odd
                ).astype(BF16)

        @pl.loop(0, 2)
        def _(h):
            half = lax.rem(lat // 16 + 1 + h, 2)
            rows = pl.ds(pl.multiple_of(half * 512, 512), 512)
            product = nt_dot(trig[rows, :], xa[first * 128:(first + count) * 128, :])
            product = (product * (1.0 / math.sqrt(NLON))).astype(BF16)
            for g in range(count):
                sb[first + g, pl.ds(half * 16, 16)] = product[
                    :, g * 128:(g + 1) * 128
                ].reshape(16, 32, 128)

            @pl.loop(0, 16)
            def _(k):
                peer = half * 16 + lax.rem(lat + k + 8, 16)

                @pl.when(peer != lat)
                def _():
                    pltpu.make_async_remote_copy(
                        src_ref=sb.at[pl.ds(first, count), peer],
                        dst_ref=zb.at[pl.ds(first, count), lat],
                        send_sem=zy_send, recv_sem=zy_recv.at[c],
                        device_id=(peer, lon), device_id_type=MESH,
                    ).start()

        for g in range(first, first + count):
            zb[g, lat] = sb[g, lat]

    def deliver(c):
        first, count = CHUNKS[c]
        window = sb.at[pl.ds(first, count), pl.ds(0, 31)]
        pltpu.make_async_copy(window, window, zy_recv.at[c]).wait()
        for g in range(first, first + count):
            @pl.loop(0, 8)
            def _(s):
                for e in range(4):
                    rows = zb[g, s * 4 + e].astype(F32)
                    for rp in range(4):
                        r32[pl.ds(s * 16 + e * 4 + rp, 8, stride=136), :] = rows[
                            rp * 8:(rp + 1) * 8
                        ]

            for j in range(8):
                rbs[g, j] = r32[j * 136:j * 136 + 128, :].astype(BF16)

        @pl.loop(1, 8)
        def _(k):
            peer = lax.rem(lon + k, 8)
            pltpu.make_async_remote_copy(
                src_ref=rbs.at[pl.ds(first, count), peer],
                dst_ref=rb.at[pl.ds(first, count), lon],
                send_sem=s2_send, recv_sem=s2_recv.at[c],
                device_id=(lat, peer), device_id_type=MESH,
            ).start()

        for g in range(first, first + count):
            rb[g, lon] = rbs[g, lon]

    slot = (lat * 8 + lon) * 2

    def collect(c):
        first, count = CHUNKS[c]
        window = rb.at[pl.ds(first, count), pl.ds(0, 7)]
        pltpu.make_async_copy(window, window, s2_recv.at[c]).wait()
        for g in range(first, first + count):
            @pl.loop(0, 8)
            def _(j):
                c32[pl.ds(pl.multiple_of(j * 128, 128), 128), :] = rb[g, j].astype(F32)

            for r in range(2):
                for p in range(2):
                    ext32[0:128, :] = jnp.transpose(c32[pl.ds(r * 2 + p, 256, stride=4), :])
                    for i in range(5):
                        amat[r, p, g * 32:(g + 1) * 32, i * 256:(i + 1) * 256] = ext32[
                            FG * i:FG * i + 32, :
                        ].astype(BF16)
        rows = slice(first * 32, (first + count) * 32)
        degree = lax.broadcasted_iota(jnp.int32, (count * 64, NT), 1)
        for r in range(2):
            full = jnp.dot(
                amat[r, :, rows, :].reshape(count * 64, 1280), legp[r],
                preferred_element_type=F32,
            )
            full = jnp.where(degree >= wave_ref[slot + r], full, 0.0)
            for p in range(2):
                part = full[p * count * 32:(p + 1) * count * 32]
                out[r, p, rows, :] = part
                for g in range(count):
                    start = 4 * FG * (first + g) + r * 2 + p
                    for u in range(5):
                        ost[u, pl.ds(start, 32, stride=4), :] = part[
                            g * 32:(g + 1) * 32, u * 128:(u + 1) * 128
                        ]

    analyse(0)
    analyse(1)
    analyse(2)
    analyse(3)
    deliver(0)
    analyse(4)
    deliver(1)
    deliver(2)
    analyse(5)
    deliver(3)
    collect(0)
    deliver(4)
    collect(1)
    collect(2)
    deliver(5)
    collect(3)
    collect(4)
    collect(5)

    total = jnp.zeros((192, 192), F32)
    for r in range(2):
        factor = jnp.where(wave_ref[slot + r] == 0, 1.0, 2.0).astype(F32)
        for p in range(2):
            part = out[r, p]
            total += nt_dot(part.astype(BF16), (part * (wts[...] * factor)).astype(BF16))

    total = jnp.where(same[...] > 0.5, total, 0.0)
    pick = picks[0]
    upper = picks[1]
    high = lax.Precision.HIGHEST
    half = jnp.dot(pick[0:64], total, preferred_element_type=F32, precision=high)
    packed = nt_dot(half[0:32], pick, high) + nt_dot(half[32:64], upper, high)
    gs[...] = (packed * (1.0 / (LEV * M * NT))).reshape(8, 4, 128)

    def ring(which, src, dst):
        @pl.loop(1, 8)
        def _(k):
            peer = lax.rem(lon + k, 8)
            pltpu.make_async_remote_copy(
                src_ref=src(peer), dst_ref=dst.at[lon],
                send_sem=g_send.at[which], recv_sem=g_recv.at[which],
                device_id=(lat, peer), device_id_type=MESH,
            ).start()

    ring(0, lambda peer: gs.at[peer], ga)
    ga[lon] = gs[lon]
    for u in range(5):
        spec_v[:, :, u * 128:(u + 1) * 128] = ost[u, 0:600, :].reshape(300, 2, 128).astype(BF16)
    store = pltpu.make_async_copy(spec_v, spec_ref, spec_sem)
    store.start()
    pltpu.make_async_copy(ga.at[pl.ds(0, 7)], ga.at[pl.ds(0, 7)], g_recv.at[0]).wait()
    gb[lat] = jnp.sum(ga[...], axis=0)

    @pl.loop(1, 32)
    def _(k):
        peer = lax.rem(lat + 1 + lax.rem(k + 11, 31), 32)
        pltpu.make_async_remote_copy(
            src_ref=gb.at[lat], dst_ref=gb.at[lat],
            send_sem=g_send.at[1], recv_sem=g_recv.at[1],
            device_id=(peer, lon), device_id_type=MESH,
        ).start()

    pltpu.make_async_copy(gb.at[pl.ds(0, 31)], gb.at[pl.ds(0, 31)], g_recv.at[1]).wait()
    gc[lon] = jnp.sum(gb[...], axis=0)
    ring(2, lambda peer: gc.at[lon], gc)
    pltpu.make_async_copy(gc.at[pl.ds(0, 7)], gc.at[pl.ds(0, 7)], g_recv.at[2]).wait()
    packed = gc[...].reshape(32, 128)
    gram_ref[0:32, :] = packed[:, 0:50]
    gram_ref[32:50, :] = packed[0:18, 64:114]

    store.wait()

    window = xa.at[:, pl.ds(0, 1792)]
    pltpu.make_async_copy(window, window, s1_send).wait()
    window = xrr.at[pl.ds(0, 7)]
    pltpu.make_async_copy(window, window, s1r_send).wait()
    window = sb.at[:, pl.ds(0, 31)]
    pltpu.make_async_copy(window, window, zy_send).wait()
    window = rb.at[:, pl.ds(0, 7)]
    pltpu.make_async_copy(window, window, s2_send).wait()
    pltpu.make_async_copy(ga.at[pl.ds(0, 7)], ga.at[pl.ds(0, 7)], g_send.at[0]).wait()
    pltpu.make_async_copy(gb.at[pl.ds(0, 31)], gb.at[pl.ds(0, 31)], g_send.at[1]).wait()
    pltpu.make_async_copy(gc.at[pl.ds(0, 7)], gc.at[pl.ds(0, 7)], g_send.at[2]).wait()


def hand_on(spec_in, gram_in, spec_out, gram_out, sems):
    copies = [
        pltpu.make_async_copy(gram_in, gram_out, sems.at[3]),
    ] + [
        pltpu.make_async_copy(
            spec_in.at[pl.ds(100 * b, 100)], spec_out.at[pl.ds(100 * b, 100)], sems.at[b]
        )
        for b in range(3)
    ]
    for copy in copies:
        copy.start()
    for copy in copies:
        copy.wait()


def on_device(grid_fields, legendre, wave_of_slot, energy_weight):
    rows = grid_fields.transpose(1, 2, 0, 3).reshape(150, 40, 320)
    waves = wave_of_slot.reshape(4, 128)
    vmem = pl.BlockSpec(memory_space=pltpu.VMEM)
    dma = pltpu.SemaphoreType.DMA
    many = dma((len(CHUNKS),))
    spectral, gram_matrix = pl.pallas_call(
        kernel,
        out_shape=(
            jax.ShapeDtypeStruct((300, 2, NT), BF16),
            jax.ShapeDtypeStruct((50, 50), F32),
        ),
        in_specs=[
            pl.BlockSpec(memory_space=pl.ANY),
            pl.BlockSpec(memory_space=pl.ANY),
            vmem,
            pl.BlockSpec(memory_space=pltpu.SMEM),
            vmem,
        ],
        out_specs=(pl.BlockSpec(memory_space=pl.ANY), vmem),
        scratch_shapes=[
            pltpu.VMEM((150, 40, 320), BF16),
            pltpu.VMEM((6, 3, 1008, 128), F32),
            pltpu.VMEM((8, 768, 256), BF16),
            pltpu.VMEM((8, 384, 128), BF16),
            pltpu.VMEM((768, NLON), BF16),
            pltpu.VMEM((8, 384, 128), BF16),
            pltpu.VMEM((1024, NLON), BF16),
            pltpu.VMEM((512, 128), F32),
            pltpu.VMEM((512, 128), F32),
            pltpu.VMEM((6, 32, 32, 128), BF16),
            pltpu.VMEM((6, 32, 32, 128), BF16),
            pltpu.VMEM((8 * 136, 128), F32),
            pltpu.VMEM((6, 8, 128, 128), BF16),
            pltpu.VMEM((6, 8, 128, 128), BF16),
            pltpu.VMEM((2, 1280, NT), BF16),
            pltpu.VMEM((5, 1280, 128), F32),
            pltpu.VMEM((2, 1280, NT), BF16),
            pltpu.VMEM((1024, 128), F32),
            pltpu.VMEM((136, 256), F32),
            pltpu.VMEM((2, 2, 192, 1280), BF16),
            pltpu.VMEM((2, 2, 192, NT), F32),
            pltpu.VMEM((5, 632, 128), F32),
            pltpu.VMEM((192, NT), F32),
            pltpu.VMEM((192, 192), F32),
            pltpu.VMEM((2, 128, 192), F32),
            pltpu.VMEM((300, 2, NT), BF16),
            pltpu.VMEM((8, 4, 128), F32),
            pltpu.VMEM((8, 4, 128), F32),
            pltpu.VMEM((32, 4, 128), F32),
            pltpu.VMEM((8, 4, 128), F32),
            dma((6,)), dma, dma, many, dma, many, dma, many,
            dma, many, dma, many, dma((3,)), dma((3,)),
        ],
        compiler_params=pltpu.CompilerParams(
            collective_id=0, has_side_effects=True, vmem_limit_bytes=60 * 1024 * 1024,
        ),
        cost_estimate=pl.CostEstimate(
            flops=6_000_000_000, bytes_accessed=12_000_000, transcendentals=0
        ),
    )(rows, legendre, waves, wave_of_slot, energy_weight)
    anywhere = pl.BlockSpec(memory_space=pl.ANY)
    spectral, gram_matrix = pl.pallas_call(
        hand_on,
        out_shape=(
            jax.ShapeDtypeStruct((300, 2, NT), BF16),
            jax.ShapeDtypeStruct((50, 50), F32),
        ),
        in_specs=[vmem, vmem],
        out_specs=(anywhere, anywhere),
        scratch_shapes=[dma((4,))],
    )(spectral, gram_matrix)
    return spectral.reshape(50, LEV, 2, 2, NT), gram_matrix


def solution(mesh):
    placed = (P("lat", None, None, "lon"), P(("lat", "lon"), None, None), P(), P())
    return jax.shard_map(
        on_device,
        mesh=mesh,
        in_specs=placed,
        out_specs=(P(None, None, ("lat", "lon"), None, None), P()),
        check_vma=False,
    )
```
